32 devices in a mesh: groups: 2 (over y), people: 4 (over z), blocks: 2 (over x), sub: 2 (over core).
Axes of the slice: x: 2, y: 2, z: 4, core: 2. Of those that a mesh axis runs over, the one named last changes fastest.
Arguments:
- dosage: int32 [4096, 2048], P(('groups', 'people', 'sub'), 'blocks'), parts along dimension 0, may hold values from 0 to 200
- fold: int32 [4096], P(('groups', 'people', 'sub')), parts along dimension 0, may hold values from 0 to 1, as said below
- pheno: bfloat16 [4096, 48], P(('groups', 'people', 'sub')), parts along dimension 0, may hold values from -8 to 8
- ridges: float32 [5], replicated, may hold values from 1 to 20
Outputs:
- second: float32 [48, 5, 4096], P(('blocks', 'sub'), None, ('groups', 'people')), parts along dimension 2
The draws below stay inside these ranges and needn't reach their ends.
There are 2 independent parts, one for each index of `groups`. The reference program is written for one: setup_inputs(seed, part) draws one part's arguments, and reference() takes and returns one part's arrays. A program takes and returns all parts, laid end to end along the dimension named above; an argument that names none is the same for every part. Nothing has to cross between parts.
Inputs may be any that keep to these rules, and one draw needn't show every extreme that they name: Each fold holds exactly 1024 people.
All inputs are finite; a program needn't handle non-finite values.
Results may differ from the reference program's by a relative error of at most 0.0021.
Values may be sent and summed in bfloat16 or wider, within the bound.
A program may use at most 64 MiB of HBM per device.

```python
import math
import jax
import jax.numpy as jnp
from jax import lax

BLOCK = 1024
TRAITS = 48
RIDGES = 5
FOLDS = 2
ITERS = 10
ITERS_TWO = 4
PEOPLE = 2048
NBLK = 2
VARIANTS = 2048


def dosage_table(key):
    level_key = jax.random.fold_in(key, 71)
    value_key = jax.random.fold_in(key, 73)
    levels = jax.random.randint(level_key, (VARIANTS,), 1, 41)
    levels = levels.at[:5].set(40)
    offsets = (40 - levels) // 2
    values = jax.random.randint(value_key, (PEOPLE, VARIANTS), 0, levels[None, :] + 1) + offsets[None, :]
    values = values.at[0, :5].set(40)
    values = values.at[1, :5].set(0)
    summed = values
    for shift_step in range(1, 5):
        summed = summed + jnp.roll(values, -shift_step, axis=1)
    return summed.astype(jnp.int32)


def draw_dosage(key, part):
    return dosage_table(key)


def draw_fold(key, part):
    order = jax.random.permutation(jax.random.fold_in(key, 31), PEOPLE)
    return (order % FOLDS).astype(jnp.int32)


def draw_pheno(key, part):
    centred = dosage_table(key).astype(jnp.float32) - 100.0
    effects = jax.random.normal(jax.random.fold_in(key, 11), (VARIANTS, TRAITS), jnp.float32)
    signal = jnp.dot(centred, effects)
    signal = (signal - jnp.mean(signal, 0)) / (jnp.std(signal, 0) + 1e-06)
    noise = jax.random.normal(jax.random.fold_in(key, 13), (PEOPLE, TRAITS), jnp.float32)
    heritable = jax.random.uniform(jax.random.fold_in(key, 17), (TRAITS,), jnp.float32, 0.2, 0.8)
    values = jnp.sqrt(heritable) * signal + jnp.sqrt(1.0 - heritable) * noise
    return jnp.clip(values, -8.0, 8.0).astype(jnp.bfloat16)


def setup_inputs(seed: int = 0, part: int = 0) -> dict:
    arg_keys = jax.random.split(jax.random.key(seed), 5)
    own_keys = jax.random.split(jax.random.fold_in(arg_keys[4], part), 5)
    dosage = draw_dosage(jax.random.fold_in(jax.random.fold_in(arg_keys[4], part), 71), part)
    fold = draw_fold(jax.random.fold_in(jax.random.fold_in(arg_keys[4], part), 71), part)
    pheno = draw_pheno(jax.random.fold_in(jax.random.fold_in(arg_keys[4], part), 71), part)
    ridges = jnp.clip(jnp.exp(jax.random.uniform(arg_keys[3], (RIDGES,), jnp.float32, math.log(1.0), math.log(20.0))), 1.0, 20.0)
    return dict(dosage=dosage, fold=fold, pheno=pheno, ridges=ridges)


highest = lax.Precision.HIGHEST

def conjugate(apply_system, right_side, steps):
    estimate = jnp.zeros_like(right_side)
    residual = right_side
    direction = right_side
    current = lax.optimization_barrier(jnp.sum(residual * residual, -2, keepdims=True))
    for step in range(steps):
        image = apply_system(direction)
        alpha = current / lax.optimization_barrier(jnp.sum(direction * image, -2, keepdims=True))
        estimate = estimate + alpha * direction
        residual = residual - alpha * image
        following = lax.optimization_barrier(jnp.sum(residual * residual, -2, keepdims=True))
        direction = residual + following / current * direction
        current = following
    return estimate

def covariance_rows(gram_rows, row_sums, all_sums, row_mean, all_mean, train_count):
    return gram_rows - row_sums[:, None] * all_mean[None, :] - row_mean[:, None] * all_sums[None, :] + train_count * row_mean[:, None] * all_mean[None, :]

def train_total(pieces, fold_index):
    return sum([pieces[other] for other in range(FOLDS) if other != fold_index])

def reference(dosage, fold, pheno, ridges):
    people = dosage.shape[0]
    train_count = people - people // FOLDS
    centred = (dosage - 100).astype(jnp.bfloat16)
    pheno_wide = pheno.astype(jnp.float32)
    masks = [fold[:, None] == fold_index for fold_index in range(FOLDS)]
    level_zero = []
    for block_index in range(NBLK):
        section = centred[:, block_index * BLOCK:(block_index + 1) * BLOCK]
        grams, sums, squares, cross, totals = ([], [], [], [], [])
        for mask in masks:
            masked = jnp.where(mask, section, jnp.zeros_like(section))
            grams.append(jnp.dot(masked.T, section, preferred_element_type=jnp.float32))
            masked_wide = masked.astype(jnp.float32)
            sums.append(lax.optimization_barrier(jnp.sum(masked_wide, 0)))
            squares.append(lax.optimization_barrier(jnp.sum(masked_wide * masked_wide, 0)))
            cross.append(jnp.dot(masked.T, pheno, preferred_element_type=jnp.float32))
            totals.append(lax.optimization_barrier(jnp.sum(jnp.where(mask, pheno_wide, 0.0), 0)))
        column_mean = sum(sums) / people
        column_spread = jnp.sqrt(sum(squares) / people - column_mean * column_mean + 1e-05)
        shifts = jnp.repeat(ridges, TRAITS)
        prediction = jnp.zeros((people, RIDGES * TRAITS), jnp.float32)
        for fold_index in range(FOLDS):
            sums_train = train_total(sums, fold_index)
            covariance = covariance_rows(train_total(grams, fold_index), sums_train, sums_train, column_mean, column_mean, train_count)
            system = covariance / (train_count * column_spread[:, None] * column_spread[None, :])
            right_side = (train_total(cross, fold_index) - column_mean[:, None] * train_total(totals, fold_index)[None, :]) / (train_count * column_spread[:, None])
            estimate = conjugate(lambda direction: jnp.dot(system, direction, precision=highest) + shifts * direction, jnp.tile(right_side, (1, RIDGES)), ITERS)
            scaled = (estimate / column_spread[:, None]).astype(jnp.bfloat16)
            offset = jnp.dot(column_mean, scaled.astype(jnp.float32), precision=highest)
            outcome = jnp.dot(section, scaled, preferred_element_type=jnp.float32) - offset
            prediction = prediction + jnp.where(masks[fold_index], outcome, 0.0)
        level_zero.append(prediction.astype(jnp.bfloat16).reshape(people, RIDGES, TRAITS))
    stacked = jnp.stack(level_zero, 1)
    predictors = jnp.transpose(stacked, (0, 3, 1, 2)).reshape(people, TRAITS, NBLK * RIDGES)
    predictors_wide = predictors.astype(jnp.float32)
    gram_two = jnp.einsum('nta,ntb->tab', predictors_wide, predictors_wide, precision=highest) / people
    cross_two = jnp.einsum('nt,nta->ta', pheno_wide, predictors_wide, precision=highest) / people
    level = jnp.trace(gram_two, axis1=1, axis2=2) / (NBLK * RIDGES) + 1e-06
    level_shift = ridges[None, None, :] * level[:, None, None]
    right_two = jnp.broadcast_to(cross_two[:, :, None], (TRAITS, NBLK * RIDGES, RIDGES))
    weights = conjugate(lambda direction: jnp.einsum('tab,tbr->tar', gram_two, direction, precision=highest) + level_shift * direction, right_two, ITERS_TWO)
    return jnp.einsum('nta,tar->trn', predictors_wide, weights, precision=highest)
```

```python
import functools

import jax
import jax.numpy as jnp
import numpy as np
from jax import lax
from jax.experimental import pallas as pl
from jax.experimental.pallas import tpu as pltpu
from jax.sharding import PartitionSpec as P

TRAITS = 48
RIDGES = 5
FOLDS = 2
ITERS = 10
ITERS_TWO = 4
AUX = 64
FOLD_ROW = 48
ONE_ROW = 49

MESH = pl.DeviceIdType.MESH
F32 = jnp.float32
BF16 = jnp.bfloat16
NT = (((1,), (1,)), ((), ()))
highest = lax.Precision.HIGHEST


def dot_nt(left, right, precision=None):
    return lax.dot_general(left, right, NT, precision=precision, preferred_element_type=F32)


def kernel(
    sizes,
    dosage, aux, colinfo, perm, ridges,
    out,
    slots, pair, gram, system_hi, system_lo, cross, plain, row_train, row_all, totals, square,
    estimate, residual, direction, split, image, turned, pred, moved, packed, reduced,
    slot_send, slot_recv, forward_send, pair_send, pair_recv,
    pred_send, pred_recv, red_send, red_recv,
):
    depth, lines, share, half, pitch, people = sizes
    rows, block = dosage.shape
    columns = estimate.shape[1]
    train_count = float(people - people // FOLDS)
    z = lax.axis_index("people")
    x = lax.axis_index("blocks")
    core = lax.axis_index("sub")
    other = 1 - core
    total = depth * lines * 2
    me = (z * lines + x) * 2 + core

    barrier = pltpu.get_barrier_semaphore()

    @pl.loop(0, total)
    def _(index):
        @pl.when(index != me)
        def _():
            pl.semaphore_signal(
                barrier, inc=1,
                device_id={
                    "people": index // (lines * 2),
                    "blocks": (index // 2) % lines,
                    "sub": index % 2,
                },
                device_id_type=MESH,
            )

    mine = 2 * z + core
    slots[mine, pl.ds(0, block), :] = (
        jnp.transpose((dosage[...] - 100).astype(F32)).astype(BF16)
    )
    slots[mine, pl.ds(block, AUX), :] = aux[...]
    pair[core] = aux[...]
    pl.semaphore_wait(barrier, total - 1)

    first = depth // 2 - 1
    near = (z >= depth // 2).astype(jnp.int32)

    def slot_copy(place, send_sem, target):
        return pltpu.make_async_remote_copy(
            src_ref=slots.at[place], dst_ref=slots.at[place],
            send_sem=send_sem, recv_sem=slot_recv.at[place],
            device_id=target, device_id_type=MESH,
        )

    for order in range(2):
        goal = first + (near if order == 0 else 1 - near)

        @pl.when(z != goal)
        def _():
            slot_copy(mine, slot_send.at[order], {"people": goal}).start()

    pair_copy = pltpu.make_async_remote_copy(
        src_ref=pair.at[core], dst_ref=pair.at[core],
        send_sem=pair_send, recv_sem=pair_recv,
        device_id={"sub": other}, device_id_type=MESH,
    )
    pair_copy.start()

    solver = z - first
    is_solver = (solver >= 0) & (solver < 2)

    def pred_copy(far, group):
        return pltpu.make_async_remote_copy(
            src_ref=pred.at[far, pl.ds(group * pitch, pitch), :],
            dst_ref=moved.at[x, solver, core],
            send_sem=pred_send.at[far, group],
            recv_sem=pred_recv.at[x, solver, core],
            device_id={"people": far, "blocks": group // 2, "sub": group % 2},
            device_id_type=MESH,
        )

    @pl.when(is_solver)
    def _():
        gram[...] = jnp.zeros_like(gram)
        cross[...] = jnp.zeros_like(cross)
        plain[...] = jnp.zeros_like(plain)
        row_train[...] = jnp.zeros_like(row_train)
        row_all[...] = jnp.zeros_like(row_all)
        totals[...] = jnp.zeros_like(totals)
        square[...] = jnp.zeros_like(square)
        sign = 1 - 2 * solver

        @pl.loop(0, 2 * depth)
        def _(step):
            turn = step // 2
            late = step % 2
            far = z + sign * ((turn + 1) // 2) * (2 * (turn % 2) - 1)
            place = 2 * far + jnp.where(late == 0, core, other)
            copy = slot_copy(place, forward_send.at[far], {"sub": other})

            @pl.when(step > 0)
            def _():
                copy.wait_recv()

            @pl.when(late == 0)
            def _():
                copy.start()

            extra = slots[place, pl.ds(block, AUX), :]
            tail = slots[place, pl.ds(block + FOLD_ROW, AUX - FOLD_ROW), :]
            keep = (tail[0:1, :].astype(F32) != core.astype(F32)).astype(F32).astype(BF16)
            whole = slots[place, pl.ds(0, block), :]
            tile = 256
            for part in range(block // tile):
                span = pl.ds(part * tile, tile)
                own = slots[place, span, :]
                masked = own * keep
                gram[span, :] += dot_nt(masked, whole)
                cross[span, :] += dot_nt(masked, extra)
                plain[span, :] += dot_nt(own, extra)
                row_train[:, span] += dot_nt(tail, masked)
                row_all[:, span] += dot_nt(tail, own)
                wide = own.astype(F32)
                wide = wide * wide
                added = wide[:, 0:128]
                for lane in range(1, rows // 128):
                    added = added + wide[:, lane * 128:(lane + 1) * 128]
                square[span, :] += added
            totals[...] += dot_nt(tail * keep, extra)

        one = ONE_ROW - FOLD_ROW
        mean_row = row_all[one:one + 1, :] / people
        train_row = row_train[one:one + 1, :]
        square_row = dot_nt(jnp.ones((8, 128), F32), square[...], highest)[0:1, :]
        inverse_row = 1.0 / jnp.sqrt(square_row / people - mean_row * mean_row + 1e-05)
        shifted_row = train_row - train_count * mean_row
        pick = (
            lax.broadcasted_iota(jnp.int32, (AUX, columns), 0)
            == colinfo[0:1, :] + solver * half
        ).astype(F32)
        which = colinfo[1:2, :]
        shifts = jnp.zeros((1, columns), F32)
        for ridge in range(RIDGES):
            shifts = shifts + jnp.where(which == ridge, ridges[ridge], 0.0)
        totals_row = jnp.dot(
            totals[...], pick, precision=highest, preferred_element_type=F32
        )[one:one + 1, :]
        tile = 128
        current = jnp.zeros((1, columns), F32)
        for part in range(block // tile):
            span = pl.ds(part * tile, tile)
            mean_col = plain[span, ONE_ROW:ONE_ROW + 1] / people
            train_col = cross[span, ONE_ROW:ONE_ROW + 1]
            square_col = jnp.sum(square[span, :], 1, keepdims=True)
            spread_col = jnp.sqrt(square_col / people - mean_col * mean_col + 1e-05)
            scale_col = 1.0 / (train_count * spread_col)
            value = gram[span, :] - train_col * mean_row - mean_col * shifted_row
            value = value * scale_col * inverse_row
            high = value.astype(BF16)
            system_hi[span, :] = high
            system_lo[span, :] = (value - high.astype(F32)).astype(BF16)
            right = jnp.dot(
                cross[span, :], pick, precision=highest, preferred_element_type=F32
            )
            right = (right - mean_col * totals_row) * scale_col
            residual[span, :] = right
            direction[span, :] = right
            estimate[span, :] = jnp.zeros_like(right)
            high = right.astype(BF16)
            split[span, 0:columns] = high
            split[span, columns:2 * columns] = (right - high.astype(F32)).astype(BF16)
            current = current + jnp.sum(right * right, 0, keepdims=True)

        tile = 256

        def step(_, current):
            both = split[...]
            leading = split[:, 0:columns]
            curve = jnp.zeros((1, columns), F32)
            for part in range(block // tile):
                span = pl.ds(part * tile, tile)
                wide = jnp.dot(system_hi[span, :], both, preferred_element_type=F32)
                narrow = jnp.dot(system_lo[span, :], leading, preferred_element_type=F32)
                along = direction[span, :]
                value = wide[:, 0:columns] + (wide[:, columns:] + narrow) + shifts * along
                image[span, :] = value
                curve = curve + jnp.sum(along * value, 0, keepdims=True)
            alpha = current / curve
            following = jnp.zeros((1, columns), F32)
            for part in range(block // tile):
                span = pl.ds(part * tile, tile)
                estimate[span, :] += alpha * direction[span, :]
                left = residual[span, :] - alpha * image[span, :]
                residual[span, :] = left
                following = following + jnp.sum(left * left, 0, keepdims=True)
            ratio = following / current
            for part in range(block // tile):
                span = pl.ds(part * tile, tile)
                along = residual[span, :] + ratio * direction[span, :]
                direction[span, :] = along
                high = along.astype(BF16)
                split[span, 0:columns] = high
                split[span, columns:2 * columns] = (along - high.astype(F32)).astype(BF16)
            return following

        lax.fori_loop(0, ITERS, step, current)

        for part in range(block // tile):
            span = pl.ds(part * tile, tile)
            mean_col = plain[span, ONE_ROW:ONE_ROW + 1] / people
            square_col = jnp.sum(square[span, :], 1, keepdims=True)
            spread_col = jnp.sqrt(square_col / people - mean_col * mean_col + 1e-05)
            image[span, :] = estimate[span, :] / spread_col
        flipped = jnp.transpose(image[...]).astype(BF16)
        turned[...] = flipped
        offset = jnp.sum(flipped.astype(F32) * mean_row, 1, keepdims=True)

        @pl.loop(0, depth)
        def _(far):
            for side in range(2):
                place = 2 * far + side
                outcome = jnp.dot(
                    turned[...], slots[place, pl.ds(0, block), :], preferred_element_type=F32
                )
                tail = slots[place, pl.ds(block + FOLD_ROW, AUX - FOLD_ROW), :]
                held = tail[0:1, :].astype(F32) == core.astype(F32)
                pred[far, :, side * rows:(side + 1) * rows] = jnp.where(
                    held, outcome - offset, 0.0
                ).astype(BF16)
            for group in range(2 * lines):
                self_here = (far == z) & (x == group // 2) & (core == group % 2)

                @pl.when(self_here)
                def _():
                    moved[x, solver, core] = pred[far, group * pitch:(group + 1) * pitch, :]

                @pl.when(jnp.logical_not(self_here))
                def _():
                    pred_copy(far, group).start()

    pair_copy.wait()
    for line in range(lines):
        for which_solver in range(2):
            for side in range(2):
                self_here = (z == first + which_solver) & (x == line) & (core == side)

                @pl.when(jnp.logical_not(self_here))
                def _():
                    pltpu.make_async_remote_copy(
                        src_ref=moved.at[line, which_solver, side],
                        dst_ref=moved.at[line, which_solver, side],
                        send_sem=red_send.at[0],
                        recv_sem=pred_recv.at[line, which_solver, side],
                        device_id={"sub": other}, device_id_type=MESH,
                    ).wait_recv()

    group = x * 2 + core
    choose = (
        (lax.broadcasted_iota(jnp.int32, (16, AUX), 1)
         == group * share + lax.broadcasted_iota(jnp.int32, (16, AUX), 0))
        & (lax.broadcasted_iota(jnp.int32, (16, AUX), 0) < share)
    ).astype(F32).astype(BF16)
    target = jnp.concatenate(
        [jnp.dot(choose, pair[side], preferred_element_type=F32) for side in range(2)], 1
    )
    predictors = []
    for line in range(lines):
        stacked = jnp.concatenate(
            [moved[line, which, 0] + moved[line, which, 1] for which in range(2)], 0
        )
        ordered = jnp.dot(perm[...], stacked, preferred_element_type=F32)
        for ridge in range(RIDGES):
            predictors.append(ordered[ridge * 16:(ridge + 1) * 16, :])
    count = len(predictors)
    pairs = [(a, b) for a in range(count) for b in range(a, count)]
    width = packed.shape[1]
    lane = lax.broadcasted_iota(jnp.int32, (16, width), 1)
    gathered = jnp.zeros((16, width), F32)
    for index, (a, b) in enumerate(pairs + [(a, None) for a in range(count)]):
        product = predictors[a] * (target if b is None else predictors[b])
        gathered = jnp.where(lane == index, jnp.sum(product, 1, keepdims=True), gathered)
    packed[...] = gathered

    def red_copy(far):
        return pltpu.make_async_remote_copy(
            src_ref=packed, dst_ref=reduced.at[z],
            send_sem=red_send.at[far], recv_sem=red_recv.at[z],
            device_id={"people": far}, device_id_type=MESH,
        )

    reduced[z] = gathered
    for far in range(depth):
        @pl.when(z != far)
        def _():
            red_copy(far).start()
    for far in range(depth):
        @pl.when(z != far)
        def _():
            pltpu.make_async_remote_copy(
                src_ref=packed, dst_ref=reduced.at[far],
                send_sem=red_send.at[far], recv_sem=red_recv.at[far],
                device_id={"people": far}, device_id_type=MESH,
            ).wait_recv()
    summed = reduced[0]
    for far in range(1, depth):
        summed = summed + reduced[far]
    summed = summed / people
    small = {}
    for index, (a, b) in enumerate(pairs):
        small[a, b] = jnp.broadcast_to(summed[:, index:index + 1], (16, 128))
        small[b, a] = small[a, b]
    level = small[0, 0]
    for a in range(1, count):
        level = level + small[a, a]
    level = level / count + 1e-06
    ridge_lane = lax.broadcasted_iota(jnp.int32, (16, 128), 1)
    ridge_row = jnp.zeros((16, 128), F32)
    for ridge in range(RIDGES):
        ridge_row = ridge_row + jnp.where(ridge_lane == ridge, ridges[ridge], 0.0)
    lift = level * ridge_row
    base = len(pairs)
    left = [
        jnp.broadcast_to(summed[:, base + a:base + a + 1], (16, 128)) for a in range(count)
    ]
    along = list(left)
    gamma = [jnp.zeros((16, 128), F32) for _ in range(count)]
    now = sum(v * v for v in left)
    for _ in range(ITERS_TWO):
        result = [
            sum(small[a, b] * along[b] for b in range(count)) + lift * along[a]
            for a in range(count)
        ]
        alpha = now / sum(along[a] * result[a] for a in range(count))
        gamma = [gamma[a] + alpha * along[a] for a in range(count)]
        left = [left[a] - alpha * result[a] for a in range(count)]
        later = sum(v * v for v in left)
        ratio = later / now
        along = [left[a] + ratio * along[a] for a in range(count)]
        now = later
    for ridge in range(RIDGES):
        value = predictors[0] * gamma[0][:, ridge:ridge + 1]
        for a in range(1, count):
            value = value + predictors[a] * gamma[a][:, ridge:ridge + 1]
        out[ridge] = value

    for order in range(2):
        goal = first + (near if order == 0 else 1 - near)

        @pl.when(z != goal)
        def _():
            slot_copy(mine, slot_send.at[order], {"people": goal}).wait_send()

    for far in range(depth):
        @pl.when(z != far)
        def _():
            red_copy(far).wait_send()

    @pl.when(is_solver)
    def _():
        @pl.loop(0, depth)
        def _(far):
            slot_copy(2 * far + core, forward_send.at[far], {"sub": other}).wait_send()
            for group in range(2 * lines):
                self_here = (far == z) & (x == group // 2) & (core == group % 2)

                @pl.when(jnp.logical_not(self_here))
                def _():
                    pred_copy(far, group).wait_send()


def shards(dosage, fold, pheno, ridges):
    rows, block = dosage.shape
    depth = lax.axis_size("people")
    lines = lax.axis_size("blocks")
    people = rows * depth * 2
    groups = lines * 2
    share = TRAITS // groups
    half = share // 2
    pitch = -(-RIDGES * half // 16) * 16
    columns = groups * pitch
    aux = jnp.concatenate(
        [
            pheno.T,
            fold.astype(BF16)[None, :],
            jnp.ones((1, rows), BF16),
            jnp.zeros((AUX - TRAITS - 2, rows), BF16),
        ],
        0,
    )
    info = np.zeros((8, columns), np.int32)
    perm = np.zeros((RIDGES * 16, 2 * pitch), np.float32)
    for group in range(groups):
        for within in range(pitch):
            ridge, local = divmod(within, half) if within < RIDGES * half else (0, 0)
            info[0, group * pitch + within] = group * share + local
            info[1, group * pitch + within] = ridge
    for which in range(2):
        for within in range(RIDGES * half):
            ridge, local = divmod(within, half)
            perm[ridge * 16 + which * half + local, which * pitch + within] = 1.0
    count = lines * RIDGES
    width = -(-(count * (count + 1) // 2 + count) // 128) * 128
    vmem = pl.BlockSpec(memory_space=pltpu.VMEM)
    dma = pltpu.SemaphoreType.DMA
    result = pl.pallas_call(
        functools.partial(kernel, (depth, lines, share, half, pitch, people)),
        out_shape=jax.ShapeDtypeStruct((RIDGES, 16, 2 * rows), F32),
        in_specs=[vmem, vmem, vmem, vmem, pl.BlockSpec(memory_space=pltpu.SMEM)],
        out_specs=vmem,
        scratch_shapes=[
            pltpu.VMEM((2 * depth, block + AUX, rows), BF16),
            pltpu.VMEM((2, AUX, rows), BF16),
            pltpu.VMEM((block, block), F32),
            pltpu.VMEM((block, block), BF16),
            pltpu.VMEM((block, block), BF16),
            pltpu.VMEM((block, AUX), F32),
            pltpu.VMEM((block, AUX), F32),
            pltpu.VMEM((AUX - FOLD_ROW, block), F32),
            pltpu.VMEM((AUX - FOLD_ROW, block), F32),
            pltpu.VMEM((AUX - FOLD_ROW, AUX), F32),
            pltpu.VMEM((block, 128), F32),
            pltpu.VMEM((block, columns), F32),
            pltpu.VMEM((block, columns), F32),
            pltpu.VMEM((block, columns), F32),
            pltpu.VMEM((block, 2 * columns), BF16),
            pltpu.VMEM((block, columns), F32),
            pltpu.VMEM((columns, block), BF16),
            pltpu.VMEM((depth, columns, 2 * rows), BF16),
            pltpu.VMEM((lines, 2, 2, pitch, 2 * rows), BF16),
            pltpu.VMEM((16, width), F32),
            pltpu.VMEM((depth, 16, width), F32),
            dma((2,)),
            dma((2 * depth,)),
            dma((depth,)),
            dma,
            dma,
            dma((depth, groups)),
            dma((lines, 2, 2)),
            dma((depth,)),
            dma((depth,)),
        ],
        compiler_params=pltpu.CompilerParams(
            collective_id=0, has_side_effects=True, vmem_limit_bytes=56 * 1024 * 1024
        ),
    )(dosage, aux, jnp.asarray(info), jnp.asarray(perm, BF16), ridges)
    return jnp.transpose(result[:, :share, :], (1, 0, 2))


def solution(mesh):
    return jax.shard_map(
        shards,
        mesh=mesh,
        in_specs=(
            P(("groups", "people", "sub"), "blocks"),
            P(("groups", "people", "sub")),
            P(("groups", "people", "sub"), None),
            P(),
        ),
        out_specs=P(("blocks", "sub"), None, ("groups", "people")),
        check_vma=False,
    )
```

```python
import functools

import jax
import jax.numpy as jnp
import numpy as np
from jax import lax
from jax.experimental import pallas as pl
from jax.experimental.pallas import tpu as pltpu
from jax.sharding import PartitionSpec as P

TRAITS = 48
RIDGES = 5
FOLDS = 2
ITERS = 10
ITERS_TWO = 4
AUX = 64
FOLD_ROW = 48
ONE_ROW = 49

MESH = pl.DeviceIdType.MESH
F32 = jnp.float32
BF16 = jnp.bfloat16
NT = (((1,), (1,)), ((), ()))
highest = lax.Precision.HIGHEST


def dot_nt(left, right, precision=None):
    return lax.dot_general(left, right, NT, precision=precision, preferred_element_type=F32)


def kernel(
    sizes,
    dosage, aux, colinfo, perm, ridges,
    out,
    slots, pair, gram, system_hi, system_lo, cross, plain, totals, square,
    estimate, residual, direction, split, image, turned, pred, moved, packed, reduced,
    slot_send, slot_recv, forward_send, pair_send, pair_recv,
    pred_send, pred_recv, red_send, red_recv,
):
    depth, lines, share, half, pitch, people = sizes
    rows, block = dosage.shape
    columns = estimate.shape[1]
    train_count = float(people - people // FOLDS)
    z = lax.axis_index("people")
    x = lax.axis_index("blocks")
    core = lax.axis_index("sub")
    other = 1 - core
    total = depth * lines * 2
    me = (z * lines + x) * 2 + core

    barrier = pltpu.get_barrier_semaphore()

    @pl.loop(0, total)
    def _(index):
        @pl.when(index != me)
        def _():
            pl.semaphore_signal(
                barrier, inc=1,
                device_id={
                    "people": index // (lines * 2),
                    "blocks": (index // 2) % lines,
                    "sub": index % 2,
                },
                device_id_type=MESH,
            )

    mine = 2 * z + core
    slots[mine, pl.ds(0, block), :] = (
        jnp.transpose((dosage[...] - 100).astype(F32)).astype(BF16)
    )
    slots[mine, pl.ds(block, AUX), :] = aux[...]
    pair[core] = aux[...]
    pl.semaphore_wait(barrier, total - 1)

    first = depth // 2 - 1
    near = (z >= depth // 2).astype(jnp.int32)

    def slot_copy(place, send_sem, target):
        return pltpu.make_async_remote_copy(
            src_ref=slots.at[place], dst_ref=slots.at[place],
            send_sem=send_sem, recv_sem=slot_recv.at[place],
            device_id=target, device_id_type=MESH,
        )

    pair_copy = pltpu.make_async_remote_copy(
        src_ref=pair.at[core], dst_ref=pair.at[core],
        send_sem=pair_send, recv_sem=pair_recv,
        device_id={"sub": other}, device_id_type=MESH,
    )
    pair_copy.start()

    for order in range(2):
        goal = first + (near if order == 0 else 1 - near)

        if order == 1:
            closest = first + near

            @pl.when(z != closest)
            def _():
                slot_copy(mine, slot_send.at[0], {"people": closest}).wait_send()

        @pl.when(z != goal)
        def _():
            slot_copy(mine, slot_send.at[order], {"people": goal}).start()

    solver = z - first
    is_solver = (solver >= 0) & (solver < 2)

    def pred_copy(far, group):
        return pltpu.make_async_remote_copy(
            src_ref=pred.at[far, pl.ds(group * pitch, pitch), :],
            dst_ref=moved.at[x, solver, core],
            send_sem=pred_send.at[far, group],
            recv_sem=pred_recv.at[x, solver, core],
            device_id={"people": far, "blocks": group // 2, "sub": group % 2},
            device_id_type=MESH,
        )

    @pl.when(is_solver)
    def _():
        gram[...] = jnp.zeros_like(gram)
        cross[...] = jnp.zeros_like(cross)
        plain[...] = jnp.zeros_like(plain)
        totals[...] = jnp.zeros_like(totals)
        square[...] = jnp.zeros_like(square)
        sign = 1 - 2 * solver

        @pl.loop(0, 2 * depth)
        def _(step):
            turn = step // 2
            late = step % 2
            far = z + sign * ((turn + 1) // 2) * (2 * (turn % 2) - 1)
            place = 2 * far + jnp.where(late == 0, core, other)
            copy = slot_copy(place, forward_send.at[far], {"sub": other})

            @pl.when(step > 0)
            def _():
                copy.wait_recv()

            @pl.when(late == 0)
            def _():
                copy.start()

            extra = slots[place, pl.ds(block, AUX), :]
            tail = slots[place, pl.ds(block + FOLD_ROW, AUX - FOLD_ROW), :]
            keep = (tail[0:1, :].astype(F32) != core.astype(F32)).astype(F32).astype(BF16)
            whole = slots[place, pl.ds(0, block), :]
            tile = 256
            for part in range(block // tile):
                span = pl.ds(part * tile, tile)
                own = slots[place, span, :]
                masked = own * keep
                gram[span, :] += dot_nt(masked, whole)
                cross[span, :] += dot_nt(masked, extra)
                plain[span, :] += dot_nt(own, extra)
                wide = own.astype(F32)
                wide = wide * wide
                added = wide[:, 0:128]
                for lane in range(1, rows // 128):
                    added = added + wide[:, lane * 128:(lane + 1) * 128]
                square[span, :] += added
            totals[...] += dot_nt(tail * keep, extra)

        one = ONE_ROW - FOLD_ROW
        lane = lax.broadcasted_iota(jnp.int32, (block, 128), 1)
        table = jnp.where(
            lane == 0,
            cross[:, ONE_ROW:ONE_ROW + 1],
            jnp.where(
                lane == 1,
                plain[:, ONE_ROW:ONE_ROW + 1],
                jnp.sum(square[...], 1, keepdims=True),
            ),
        )
        table = jnp.transpose(table)
        mean_row = table[1:2, :] / people
        train_row = table[0:1, :]
        square_row = table[2:3, :]
        inverse_row = 1.0 / jnp.sqrt(square_row / people - mean_row * mean_row + 1e-05)
        shifted_row = train_row - train_count * mean_row
        pick = (
            lax.broadcasted_iota(jnp.int32, (AUX, columns), 0)
            == colinfo[0:1, :] + solver * half
        ).astype(F32)
        which = colinfo[1:2, :]
        shifts = jnp.zeros((1, columns), F32)
        for ridge in range(RIDGES):
            shifts = shifts + jnp.where(which == ridge, ridges[ridge], 0.0)
        totals_row = jnp.dot(
            totals[...], pick, precision=highest, preferred_element_type=F32
        )[one:one + 1, :]
        tile = 128
        current = jnp.zeros((1, columns), F32)
        for part in range(block // tile):
            span = pl.ds(part * tile, tile)
            mean_col = plain[span, ONE_ROW:ONE_ROW + 1] / people
            train_col = cross[span, ONE_ROW:ONE_ROW + 1]
            square_col = jnp.sum(square[span, :], 1, keepdims=True)
            spread_col = jnp.sqrt(square_col / people - mean_col * mean_col + 1e-05)
            scale_col = 1.0 / (train_count * spread_col)
            value = gram[span, :] - train_col * mean_row - mean_col * shifted_row
            value = value * scale_col * inverse_row
            high = value.astype(BF16)
            system_hi[span, :] = high
            system_lo[span, :] = (value - high.astype(F32)).astype(BF16)
            right = jnp.dot(
                cross[span, :], pick, precision=highest, preferred_element_type=F32
            )
            right = (right - mean_col * totals_row) * scale_col
            residual[span, :] = right
            direction[span, :] = right
            estimate[span, :] = jnp.zeros_like(right)
            split[span, :] = right.astype(BF16)
            current = current + jnp.sum(right * right, 0, keepdims=True)

        tile = 256

        def step(_, current):
            leading = split[...]
            curve = jnp.zeros((1, columns), F32)
            for part in range(block // tile):
                span = pl.ds(part * tile, tile)
                wide = jnp.dot(system_hi[span, :], leading, preferred_element_type=F32)
                narrow = jnp.dot(system_lo[span, :], leading, preferred_element_type=F32)
                along = direction[span, :]
                value = wide + narrow + shifts * along
                image[span, :] = value
                curve = curve + jnp.sum(along * value, 0, keepdims=True)
            alpha = current / curve
            following = jnp.zeros((1, columns), F32)
            for part in range(block // tile):
                span = pl.ds(part * tile, tile)
                estimate[span, :] += alpha * direction[span, :]
                left = residual[span, :] - alpha * image[span, :]
                residual[span, :] = left
                following = following + jnp.sum(left * left, 0, keepdims=True)
            ratio = following / current
            for part in range(block // tile):
                span = pl.ds(part * tile, tile)
                along = residual[span, :] + ratio * direction[span, :]
                direction[span, :] = along
                split[span, :] = along.astype(BF16)
            return following

        lax.fori_loop(0, ITERS, step, current)

        for part in range(block // tile):
            span = pl.ds(part * tile, tile)
            mean_col = plain[span, ONE_ROW:ONE_ROW + 1] / people
            square_col = jnp.sum(square[span, :], 1, keepdims=True)
            spread_col = jnp.sqrt(square_col / people - mean_col * mean_col + 1e-05)
            image[span, :] = estimate[span, :] / spread_col
        flipped = jnp.transpose(image[...]).astype(BF16)
        turned[...] = flipped
        offset = jnp.sum(flipped.astype(F32) * mean_row, 1, keepdims=True)

        @pl.loop(0, depth)
        def _(far):
            for side in range(2):
                place = 2 * far + side
                outcome = jnp.dot(
                    turned[...], slots[place, pl.ds(0, block), :], preferred_element_type=F32
                )
                tail = slots[place, pl.ds(block + FOLD_ROW, AUX - FOLD_ROW), :]
                held = tail[0:1, :].astype(F32) == core.astype(F32)
                pred[far, :, side * rows:(side + 1) * rows] = jnp.where(
                    held, outcome - offset, 0.0
                ).astype(BF16)
            for group in range(2 * lines):
                self_here = (far == z) & (x == group // 2) & (core == group % 2)

                @pl.when(self_here)
                def _():
                    moved[x, solver, core] = pred[far, group * pitch:(group + 1) * pitch, :]

                @pl.when(jnp.logical_not(self_here))
                def _():
                    pred_copy(far, group).start()

    pair_copy.wait()
    for line in range(lines):
        for which_solver in range(2):
            for side in range(2):
                self_here = (z == first + which_solver) & (x == line) & (core == side)

                @pl.when(jnp.logical_not(self_here))
                def _():
                    pltpu.make_async_remote_copy(
                        src_ref=moved.at[line, which_solver, side],
                        dst_ref=moved.at[line, which_solver, side],
                        send_sem=red_send.at[0],
                        recv_sem=pred_recv.at[line, which_solver, side],
                        device_id={"sub": other}, device_id_type=MESH,
                    ).wait_recv()

    group = x * 2 + core
    choose = (
        (lax.broadcasted_iota(jnp.int32, (16, AUX), 1)
         == group * share + lax.broadcasted_iota(jnp.int32, (16, AUX), 0))
        & (lax.broadcasted_iota(jnp.int32, (16, AUX), 0) < share)
    ).astype(F32).astype(BF16)
    target = jnp.concatenate(
        [jnp.dot(choose, pair[side], preferred_element_type=F32) for side in range(2)], 1
    )
    predictors = []
    for line in range(lines):
        stacked = jnp.concatenate(
            [moved[line, which, 0] + moved[line, which, 1] for which in range(2)], 0
        )
        ordered = jnp.dot(perm[...], stacked, preferred_element_type=F32)
        for ridge in range(RIDGES):
            predictors.append(ordered[ridge * 16:(ridge + 1) * 16, :])
    count = len(predictors)
    pairs = [(a, b) for a in range(count) for b in range(a, count)]
    width = packed.shape[1]
    lane = lax.broadcasted_iota(jnp.int32, (16, width), 1)
    gathered = jnp.zeros((16, width), F32)
    for index, (a, b) in enumerate(pairs + [(a, None) for a in range(count)]):
        product = predictors[a] * (target if b is None else predictors[b])
        gathered = jnp.where(lane == index, jnp.sum(product, 1, keepdims=True), gathered)
    packed[...] = gathered

    def red_copy(far):
        return pltpu.make_async_remote_copy(
            src_ref=packed, dst_ref=reduced.at[z],
            send_sem=red_send.at[far], recv_sem=red_recv.at[z],
            device_id={"people": far}, device_id_type=MESH,
        )

    reduced[z] = gathered
    for far in range(depth):
        @pl.when(z != far)
        def _():
            red_copy(far).start()
    for far in range(depth):
        @pl.when(z != far)
        def _():
            pltpu.make_async_remote_copy(
                src_ref=packed, dst_ref=reduced.at[far],
                send_sem=red_send.at[far], recv_sem=red_recv.at[far],
                device_id={"people": far}, device_id_type=MESH,
            ).wait_recv()
    summed = reduced[0]
    for far in range(1, depth):
        summed = summed + reduced[far]
    summed = summed / people
    small = {}
    for index, (a, b) in enumerate(pairs):
        small[a, b] = jnp.broadcast_to(summed[:, index:index + 1], (16, 128))
        small[b, a] = small[a, b]
    level = small[0, 0]
    for a in range(1, count):
        level = level + small[a, a]
    level = level / count + 1e-06
    ridge_lane = lax.broadcasted_iota(jnp.int32, (16, 128), 1)
    ridge_row = jnp.zeros((16, 128), F32)
    for ridge in range(RIDGES):
        ridge_row = ridge_row + jnp.where(ridge_lane == ridge, ridges[ridge], 0.0)
    lift = level * ridge_row
    base = len(pairs)
    left = [
        jnp.broadcast_to(summed[:, base + a:base + a + 1], (16, 128)) for a in range(count)
    ]
    along = list(left)
    gamma = [jnp.zeros((16, 128), F32) for _ in range(count)]
    now = sum(v * v for v in left)
    for _ in range(ITERS_TWO):
        result = [
            sum(small[a, b] * along[b] for b in range(count)) + lift * along[a]
            for a in range(count)
        ]
        alpha = now / sum(along[a] * result[a] for a in range(count))
        gamma = [gamma[a] + alpha * along[a] for a in range(count)]
        left = [left[a] - alpha * result[a] for a in range(count)]
        later = sum(v * v for v in left)
        ratio = later / now
        along = [left[a] + ratio * along[a] for a in range(count)]
        now = later
    for ridge in range(RIDGES):
        value = predictors[0] * gamma[0][:, ridge:ridge + 1]
        for a in range(1, count):
            value = value + predictors[a] * gamma[a][:, ridge:ridge + 1]
        out[ridge] = value

    furthest = first + 1 - near

    @pl.when(z != furthest)
    def _():
        slot_copy(mine, slot_send.at[1], {"people": furthest}).wait_send()

    for far in range(depth):
        @pl.when(z != far)
        def _():
            red_copy(far).wait_send()

    @pl.when(is_solver)
    def _():
        @pl.loop(0, depth)
        def _(far):
            slot_copy(2 * far + core, forward_send.at[far], {"sub": other}).wait_send()
            for group in range(2 * lines):
                self_here = (far == z) & (x == group // 2) & (core == group % 2)

                @pl.when(jnp.logical_not(self_here))
                def _():
                    pred_copy(far, group).wait_send()


def shards(dosage, fold, pheno, ridges):
    rows, block = dosage.shape
    depth = lax.axis_size("people")
    lines = lax.axis_size("blocks")
    people = rows * depth * 2
    groups = lines * 2
    share = TRAITS // groups
    half = share // 2
    pitch = -(-RIDGES * half // 16) * 16
    columns = groups * pitch
    aux = jnp.concatenate(
        [
            pheno.T,
            fold.astype(BF16)[None, :],
            jnp.ones((1, rows), BF16),
            jnp.zeros((AUX - TRAITS - 2, rows), BF16),
        ],
        0,
    )
    info = np.zeros((8, columns), np.int32)
    perm = np.zeros((RIDGES * 16, 2 * pitch), np.float32)
    for group in range(groups):
        for within in range(pitch):
            ridge, local = divmod(within, half) if within < RIDGES * half else (0, 0)
            info[0, group * pitch + within] = group * share + local
            info[1, group * pitch + within] = ridge
    for which in range(2):
        for within in range(RIDGES * half):
            ridge, local = divmod(within, half)
            perm[ridge * 16 + which * half + local, which * pitch + within] = 1.0
    count = lines * RIDGES
    width = -(-(count * (count + 1) // 2 + count) // 128) * 128
    vmem = pl.BlockSpec(memory_space=pltpu.VMEM)
    dma = pltpu.SemaphoreType.DMA
    result = pl.pallas_call(
        functools.partial(kernel, (depth, lines, share, half, pitch, people)),
        out_shape=jax.ShapeDtypeStruct((RIDGES, 16, 2 * rows), F32),
        in_specs=[vmem, vmem, vmem, vmem, pl.BlockSpec(memory_space=pltpu.SMEM)],
        out_specs=vmem,
        scratch_shapes=[
            pltpu.VMEM((2 * depth, block + AUX, rows), BF16),
            pltpu.VMEM((2, AUX, rows), BF16),
            pltpu.VMEM((block, block), F32),
            pltpu.VMEM((block, block), BF16),
            pltpu.VMEM((block, block), BF16),
            pltpu.VMEM((block, AUX), F32),
            pltpu.VMEM((block, AUX), F32),
            pltpu.VMEM((AUX - FOLD_ROW, AUX), F32),
            pltpu.VMEM((block, 128), F32),
            pltpu.VMEM((block, columns), F32),
            pltpu.VMEM((block, columns), F32),
            pltpu.VMEM((block, columns), F32),
            pltpu.VMEM((block, columns), BF16),
            pltpu.VMEM((block, columns), F32),
            pltpu.VMEM((columns, block), BF16),
            pltpu.VMEM((depth, columns, 2 * rows), BF16),
            pltpu.VMEM((lines, 2, 2, pitch, 2 * rows), BF16),
            pltpu.VMEM((16, width), F32),
            pltpu.VMEM((depth, 16, width), F32),
            dma((2,)),
            dma((2 * depth,)),
            dma((depth,)),
            dma,
            dma,
            dma((depth, groups)),
            dma((lines, 2, 2)),
            dma((depth,)),
            dma((depth,)),
        ],
        compiler_params=pltpu.CompilerParams(
            collective_id=0, has_side_effects=True, vmem_limit_bytes=56 * 1024 * 1024
        ),
    )(dosage, aux, jnp.asarray(info), jnp.asarray(perm, BF16), ridges)
    return jnp.transpose(result[:, :share, :], (1, 0, 2))


def solution(mesh):
    return jax.shard_map(
        shards,
        mesh=mesh,
        in_specs=(
            P(("groups", "people", "sub"), "blocks"),
            P(("groups", "people", "sub")),
            P(("groups", "people", "sub"), None),
            P(),
        ),
        out_specs=P(("blocks", "sub"), None, ("groups", "people")),
        check_vma=False,
    )
```

```python
import functools

import jax
import jax.numpy as jnp
import numpy as np
from jax import lax
from jax.experimental import pallas as pl
from jax.experimental.pallas import tpu as pltpu
from jax.sharding import PartitionSpec as P

TRAITS = 48
RIDGES = 5
FOLDS = 2
ITERS = 10
ITERS_TWO = 4
EXACT = 4
AUX = 64
FOLD_ROW = 48
ONE_ROW = 49

MESH = pl.DeviceIdType.MESH
F32 = jnp.float32
BF16 = jnp.bfloat16
NT = (((1,), (1,)), ((), ()))
highest = lax.Precision.HIGHEST


def dot_nt(left, right, precision=None):
    return lax.dot_general(left, right, NT, precision=precision, preferred_element_type=F32)


def kernel(
    sizes,
    dosage, fold, pheno, colinfo, perm, ridges,
    out,
    slots, wide_pheno, pair, gram, system_hi, system_lo, cross, plain, totals, square,
    estimate, residual, direction, split, image, turned, pred, moved, packed, reduced,
    slot_send, slot_recv, forward_send, pair_send, pair_recv,
    pred_send, pred_recv, red_send, red_recv,
):
    depth, lines, share, half, pitch, people = sizes
    rows, block = dosage.shape
    columns = estimate.shape[1]
    train_count = float(people - people // FOLDS)
    z = lax.axis_index("people")
    x = lax.axis_index("blocks")
    core = lax.axis_index("sub")
    other = 1 - core
    total = depth * lines * 2
    me = (z * lines + x) * 2 + core

    barrier = pltpu.get_barrier_semaphore()

    @pl.loop(0, total)
    def _(index):
        @pl.when(index != me)
        def _():
            pl.semaphore_signal(
                barrier, inc=1,
                device_id={
                    "people": index // (lines * 2),
                    "blocks": (index // 2) % lines,
                    "sub": index % 2,
                },
                device_id_type=MESH,
            )

    mine = 2 * z + core
    slots[mine, pl.ds(0, block), :] = (
        jnp.transpose((dosage[...] - 100).astype(F32)).astype(BF16)
    )
    wide_pheno[...] = jnp.zeros_like(wide_pheno)
    wide_pheno[:, 0:TRAITS] = pheno[...].astype(F32)
    row = lax.broadcasted_iota(jnp.int32, (AUX, rows), 0)
    aux = jnp.where(
        row == FOLD_ROW,
        fold[...].astype(F32),
        jnp.where(row == ONE_ROW, 1.0, jnp.transpose(wide_pheno[...])[0:AUX, :]),
    ).astype(BF16)
    slots[mine, pl.ds(block, AUX), :] = aux
    pair[core] = aux
    pl.semaphore_wait(barrier, total - 1)

    first = depth // 2 - 1
    near = (z >= depth // 2).astype(jnp.int32)

    def slot_copy(place, send_sem, target):
        return pltpu.make_async_remote_copy(
            src_ref=slots.at[place], dst_ref=slots.at[place],
            send_sem=send_sem, recv_sem=slot_recv.at[place],
            device_id=target, device_id_type=MESH,
        )

    pair_copy = pltpu.make_async_remote_copy(
        src_ref=pair.at[core], dst_ref=pair.at[core],
        send_sem=pair_send, recv_sem=pair_recv,
        device_id={"sub": other}, device_id_type=MESH,
    )
    pair_copy.start()

    for order in range(2):
        goal = first + (near if order == 0 else 1 - near)

        if order == 1:
            closest = first + near

            @pl.when(z != closest)
            def _():
                slot_copy(mine, slot_send.at[0], {"people": closest}).wait_send()

        @pl.when(z != goal)
        def _():
            slot_copy(mine, slot_send.at[order], {"people": goal}).start()

    solver = z - first
    is_solver = (solver >= 0) & (solver < 2)

    def pred_copy(far, group):
        return pltpu.make_async_remote_copy(
            src_ref=pred.at[far, pl.ds(group * pitch, pitch), :],
            dst_ref=moved.at[x, solver, core],
            send_sem=pred_send.at[far, group],
            recv_sem=pred_recv.at[x, solver, core],
            device_id={"people": far, "blocks": group // 2, "sub": group % 2},
            device_id_type=MESH,
        )

    @pl.when(is_solver)
    def _():
        gram[...] = jnp.zeros_like(gram)
        cross[...] = jnp.zeros_like(cross)
        plain[...] = jnp.zeros_like(plain)
        totals[...] = jnp.zeros_like(totals)
        square[...] = jnp.zeros_like(square)
        sign = 1 - 2 * solver

        @pl.loop(0, 2 * depth)
        def _(step):
            turn = step // 2
            late = step % 2
            far = z + sign * ((turn + 1) // 2) * (2 * (turn % 2) - 1)
            place = 2 * far + jnp.where(late == 0, core, other)
            copy = slot_copy(place, forward_send.at[far], {"sub": other})

            @pl.when(step > 0)
            def _():
                copy.wait_recv()

            @pl.when(late == 0)
            def _():
                copy.start()

            extra = slots[place, pl.ds(block, AUX), :]
            tail = slots[place, pl.ds(block + FOLD_ROW, AUX - FOLD_ROW), :]
            keep = (tail[0:1, :].astype(F32) != core.astype(F32)).astype(F32).astype(BF16)
            whole = slots[place, pl.ds(0, block), :]
            tile = 256
            for part in range(block // tile):
                span = pl.ds(part * tile, tile)
                own = slots[place, span, :]
                masked = own * keep
                gram[span, :] += dot_nt(masked, whole)
                cross[span, :] += dot_nt(masked, extra)
                plain[span, :] += dot_nt(own, extra)
                wide = own.astype(F32)
                wide = wide * wide
                added = wide[:, 0:128]
                for lane in range(1, rows // 128):
                    added = added + wide[:, lane * 128:(lane + 1) * 128]
                square[span, :] += added
            totals[...] += dot_nt(tail * keep, extra)

        one = ONE_ROW - FOLD_ROW
        lane = lax.broadcasted_iota(jnp.int32, (block, 128), 1)
        table = jnp.where(
            lane == 0,
            cross[:, ONE_ROW:ONE_ROW + 1],
            jnp.where(
                lane == 1,
                plain[:, ONE_ROW:ONE_ROW + 1],
                jnp.sum(square[...], 1, keepdims=True),
            ),
        )
        table = jnp.transpose(table)
        mean_row = table[1:2, :] / people
        train_row = table[0:1, :]
        square_row = table[2:3, :]
        inverse_row = 1.0 / jnp.sqrt(square_row / people - mean_row * mean_row + 1e-05)
        shifted_row = train_row - train_count * mean_row
        pick = (
            lax.broadcasted_iota(jnp.int32, (AUX, columns), 0)
            == colinfo[0:1, :] + solver * half
        ).astype(F32)
        which = colinfo[1:2, :]
        shifts = jnp.zeros((1, columns), F32)
        for ridge in range(RIDGES):
            shifts = shifts + jnp.where(which == ridge, ridges[ridge], 0.0)
        totals_row = jnp.dot(
            totals[...], pick, precision=highest, preferred_element_type=F32
        )[one:one + 1, :]
        tile = 128
        current = jnp.zeros((1, columns), F32)
        for part in range(block // tile):
            span = pl.ds(part * tile, tile)
            mean_col = plain[span, ONE_ROW:ONE_ROW + 1] / people
            train_col = cross[span, ONE_ROW:ONE_ROW + 1]
            square_col = jnp.sum(square[span, :], 1, keepdims=True)
            spread_col = jnp.sqrt(square_col / people - mean_col * mean_col + 1e-05)
            scale_col = 1.0 / (train_count * spread_col)
            value = gram[span, :] - train_col * mean_row - mean_col * shifted_row
            value = value * scale_col * inverse_row
            high = value.astype(BF16)
            system_hi[span, :] = high
            system_lo[span, :] = (value - high.astype(F32)).astype(BF16)
            right = jnp.dot(
                cross[span, :], pick, precision=highest, preferred_element_type=F32
            )
            right = (right - mean_col * totals_row) * scale_col
            residual[span, :] = right
            direction[span, :] = right
            estimate[span, :] = jnp.zeros_like(right)
            high = right.astype(BF16)
            split[span, 0:columns] = high
            split[span, columns:2 * columns] = (right - high.astype(F32)).astype(BF16)
            current = current + jnp.sum(right * right, 0, keepdims=True)

        tile = 256

        def step(exact, _, current):
            both = split[...] if exact else None
            leading = split[:, 0:columns]
            curve = jnp.zeros((1, columns), F32)
            for part in range(block // tile):
                span = pl.ds(part * tile, tile)
                along = direction[span, :]
                if exact:
                    wide = jnp.dot(system_hi[span, :], both, preferred_element_type=F32)
                    narrow = jnp.dot(system_lo[span, :], leading, preferred_element_type=F32)
                    value = wide[:, 0:columns] + (wide[:, columns:] + narrow)
                else:
                    value = jnp.dot(system_hi[span, :], leading, preferred_element_type=F32)
                value = value + shifts * along
                image[span, :] = value
                curve = curve + jnp.sum(along * value, 0, keepdims=True)
            alpha = current / curve
            following = jnp.zeros((1, columns), F32)
            for part in range(block // tile):
                span = pl.ds(part * tile, tile)
                left = residual[span, :] - alpha * image[span, :]
                residual[span, :] = left
                following = following + jnp.sum(left * left, 0, keepdims=True)
            ratio = following / current
            for part in range(block // tile):
                span = pl.ds(part * tile, tile)
                along = direction[span, :]
                estimate[span, :] += alpha * along
                along = residual[span, :] + ratio * along
                direction[span, :] = along
                high = along.astype(BF16)
                split[span, 0:columns] = high
                if exact:
                    split[span, columns:2 * columns] = (along - high.astype(F32)).astype(BF16)
            return following

        current = lax.fori_loop(0, EXACT, functools.partial(step, True), current)
        lax.fori_loop(EXACT, ITERS, functools.partial(step, False), current)

        for part in range(block // tile):
            span = pl.ds(part * tile, tile)
            mean_col = plain[span, ONE_ROW:ONE_ROW + 1] / people
            square_col = jnp.sum(square[span, :], 1, keepdims=True)
            spread_col = jnp.sqrt(square_col / people - mean_col * mean_col + 1e-05)
            image[span, :] = estimate[span, :] / spread_col
        flipped = jnp.transpose(image[...]).astype(BF16)
        turned[...] = flipped
        offset = jnp.sum(flipped.astype(F32) * mean_row, 1, keepdims=True)

        @pl.loop(0, depth)
        def _(far):
            for side in range(2):
                place = 2 * far + side
                outcome = jnp.dot(
                    turned[...], slots[place, pl.ds(0, block), :], preferred_element_type=F32
                )
                tail = slots[place, pl.ds(block + FOLD_ROW, AUX - FOLD_ROW), :]
                held = tail[0:1, :].astype(F32) == core.astype(F32)
                pred[far, :, side * rows:(side + 1) * rows] = jnp.where(
                    held, outcome - offset, 0.0
                ).astype(BF16)
            for group in range(2 * lines):
                self_here = (far == z) & (x == group // 2) & (core == group % 2)

                @pl.when(self_here)
                def _():
                    moved[x, solver, core] = pred[far, group * pitch:(group + 1) * pitch, :]

                @pl.when(jnp.logical_not(self_here))
                def _():
                    pred_copy(far, group).start()

    pair_copy.wait()
    for line in range(lines):
        for which_solver in range(2):
            for side in range(2):
                self_here = (z == first + which_solver) & (x == line) & (core == side)

                @pl.when(jnp.logical_not(self_here))
                def _():
                    pltpu.make_async_remote_copy(
                        src_ref=moved.at[line, which_solver, side],
                        dst_ref=moved.at[line, which_solver, side],
                        send_sem=red_send.at[0],
                        recv_sem=pred_recv.at[line, which_solver, side],
                        device_id={"sub": other}, device_id_type=MESH,
                    ).wait_recv()

    group = x * 2 + core
    choose = (
        (lax.broadcasted_iota(jnp.int32, (16, AUX), 1)
         == group * share + lax.broadcasted_iota(jnp.int32, (16, AUX), 0))
        & (lax.broadcasted_iota(jnp.int32, (16, AUX), 0) < share)
    ).astype(F32).astype(BF16)
    target = jnp.concatenate(
        [jnp.dot(choose, pair[side], preferred_element_type=F32) for side in range(2)], 1
    )
    predictors = []
    for line in range(lines):
        stacked = jnp.concatenate(
            [moved[line, which, 0] + moved[line, which, 1] for which in range(2)], 0
        )
        ordered = jnp.dot(perm[...], stacked, preferred_element_type=F32)
        for ridge in range(RIDGES):
            predictors.append(ordered[ridge * 16:(ridge + 1) * 16, :])
    count = len(predictors)
    pairs = [(a, b) for a in range(count) for b in range(a, count)]
    width = packed.shape[1]
    lane = lax.broadcasted_iota(jnp.int32, (16, width), 1)
    gathered = jnp.zeros((16, width), F32)
    for index, (a, b) in enumerate(pairs + [(a, None) for a in range(count)]):
        product = predictors[a] * (target if b is None else predictors[b])
        gathered = jnp.where(lane == index, jnp.sum(product, 1, keepdims=True), gathered)
    packed[...] = gathered

    def red_copy(far):
        return pltpu.make_async_remote_copy(
            src_ref=packed, dst_ref=reduced.at[z],
            send_sem=red_send.at[far], recv_sem=red_recv.at[z],
            device_id={"people": far}, device_id_type=MESH,
        )

    reduced[z] = gathered
    for far in range(depth):
        @pl.when(z != far)
        def _():
            red_copy(far).start()
    for far in range(depth):
        @pl.when(z != far)
        def _():
            pltpu.make_async_remote_copy(
                src_ref=packed, dst_ref=reduced.at[far],
                send_sem=red_send.at[far], recv_sem=red_recv.at[far],
                device_id={"people": far}, device_id_type=MESH,
            ).wait_recv()
    summed = reduced[0]
    for far in range(1, depth):
        summed = summed + reduced[far]
    summed = summed / people
    small = {}
    for index, (a, b) in enumerate(pairs):
        small[a, b] = jnp.broadcast_to(summed[:, index:index + 1], (16, 128))
        small[b, a] = small[a, b]
    level = small[0, 0]
    for a in range(1, count):
        level = level + small[a, a]
    level = level / count + 1e-06
    ridge_lane = lax.broadcasted_iota(jnp.int32, (16, 128), 1)
    ridge_row = jnp.zeros((16, 128), F32)
    for ridge in range(RIDGES):
        ridge_row = ridge_row + jnp.where(ridge_lane == ridge, ridges[ridge], 0.0)
    lift = level * ridge_row
    base = len(pairs)
    left = [
        jnp.broadcast_to(summed[:, base + a:base + a + 1], (16, 128)) for a in range(count)
    ]
    along = list(left)
    gamma = [jnp.zeros((16, 128), F32) for _ in range(count)]
    now = sum(v * v for v in left)
    for _ in range(ITERS_TWO):
        result = [
            sum(small[a, b] * along[b] for b in range(count)) + lift * along[a]
            for a in range(count)
        ]
        alpha = now / sum(along[a] * result[a] for a in range(count))
        gamma = [gamma[a] + alpha * along[a] for a in range(count)]
        left = [left[a] - alpha * result[a] for a in range(count)]
        later = sum(v * v for v in left)
        ratio = later / now
        along = [left[a] + ratio * along[a] for a in range(count)]
        now = later
    for ridge in range(RIDGES):
        value = predictors[0] * gamma[0][:, ridge:ridge + 1]
        for a in range(1, count):
            value = value + predictors[a] * gamma[a][:, ridge:ridge + 1]
        out[ridge] = value

    furthest = first + 1 - near

    @pl.when(z != furthest)
    def _():
        slot_copy(mine, slot_send.at[1], {"people": furthest}).wait_send()

    for far in range(depth):
        @pl.when(z != far)
        def _():
            red_copy(far).wait_send()

    @pl.when(is_solver)
    def _():
        @pl.loop(0, depth)
        def _(far):
            slot_copy(2 * far + core, forward_send.at[far], {"sub": other}).wait_send()
            for group in range(2 * lines):
                self_here = (far == z) & (x == group // 2) & (core == group % 2)

                @pl.when(jnp.logical_not(self_here))
                def _():
                    pred_copy(far, group).wait_send()


def shards(dosage, fold, pheno, ridges):
    rows, block = dosage.shape
    depth = lax.axis_size("people")
    lines = lax.axis_size("blocks")
    people = rows * depth * 2
    groups = lines * 2
    share = TRAITS // groups
    half = share // 2
    pitch = -(-RIDGES * half // 16) * 16
    columns = groups * pitch
    info = np.zeros((8, columns), np.int32)
    perm = np.zeros((RIDGES * 16, 2 * pitch), np.float32)
    for group in range(groups):
        for within in range(pitch):
            ridge, local = divmod(within, half) if within < RIDGES * half else (0, 0)
            info[0, group * pitch + within] = group * share + local
            info[1, group * pitch + within] = ridge
    for which in range(2):
        for within in range(RIDGES * half):
            ridge, local = divmod(within, half)
            perm[ridge * 16 + which * half + local, which * pitch + within] = 1.0
    count = lines * RIDGES
    width = -(-(count * (count + 1) // 2 + count) // 128) * 128
    vmem = pl.BlockSpec(memory_space=pltpu.VMEM)
    dma = pltpu.SemaphoreType.DMA
    result = pl.pallas_call(
        functools.partial(kernel, (depth, lines, share, half, pitch, people)),
        out_shape=jax.ShapeDtypeStruct((RIDGES, 16, 2 * rows), F32),
        in_specs=[vmem, vmem, vmem, vmem, vmem, pl.BlockSpec(memory_space=pltpu.SMEM)],
        out_specs=vmem,
        scratch_shapes=[
            pltpu.VMEM((2 * depth, block + AUX, rows), BF16),
            pltpu.VMEM((rows, 128), F32),
            pltpu.VMEM((2, AUX, rows), BF16),
            pltpu.VMEM((block, block), F32),
            pltpu.VMEM((block, block), BF16),
            pltpu.VMEM((block, block), BF16),
            pltpu.VMEM((block, AUX), F32),
            pltpu.VMEM((block, AUX), F32),
            pltpu.VMEM((AUX - FOLD_ROW, AUX), F32),
            pltpu.VMEM((block, 128), F32),
            pltpu.VMEM((block, columns), F32),
            pltpu.VMEM((block, columns), F32),
            pltpu.VMEM((block, columns), F32),
            pltpu.VMEM((block, 2 * columns), BF16),
            pltpu.VMEM((block, columns), F32),
            pltpu.VMEM((columns, block), BF16),
            pltpu.VMEM((depth, columns, 2 * rows), BF16),
            pltpu.VMEM((lines, 2, 2, pitch, 2 * rows), BF16),
            pltpu.VMEM((16, width), F32),
            pltpu.VMEM((depth, 16, width), F32),
            dma((2,)),
            dma((2 * depth,)),
            dma((depth,)),
            dma,
            dma,
            dma((depth, groups)),
            dma((lines, 2, 2)),
            dma((depth,)),
            dma((depth,)),
        ],
        compiler_params=pltpu.CompilerParams(
            collective_id=0, has_side_effects=True, vmem_limit_bytes=56 * 1024 * 1024
        ),
    )(dosage, fold[None, :], pheno, jnp.asarray(info), jnp.asarray(perm, BF16), ridges)
    return jnp.transpose(result[:, :share, :], (1, 0, 2))


def solution(mesh):
    return jax.shard_map(
        shards,
        mesh=mesh,
        in_specs=(
            P(("groups", "people", "sub"), "blocks"),
            P(("groups", "people", "sub")),
            P(("groups", "people", "sub"), None),
            P(),
        ),
        out_specs=P(("blocks", "sub"), None, ("groups", "people")),
        check_vma=False,
    )
```

```python
import functools

import jax
import jax.numpy as jnp
import numpy as np
from jax import lax
from jax.experimental import pallas as pl
from jax.experimental.pallas import tpu as pltpu
from jax.sharding import PartitionSpec as P

TRAITS = 48
RIDGES = 5
FOLDS = 2
ITERS = 10
ITERS_TWO = 4
EXACT = 4
PIECES = 4
AUX = 64
FOLD_ROW = 48
ONE_ROW = 49

MESH = pl.DeviceIdType.MESH
F32 = jnp.float32
BF16 = jnp.bfloat16
NT = (((1,), (1,)), ((), ()))
highest = lax.Precision.HIGHEST


def dot_nt(left, right, precision=None):
    return lax.dot_general(left, right, NT, precision=precision, preferred_element_type=F32)


def kernel(
    sizes,
    dosage, fold, pheno, colinfo, perm, ridges,
    out,
    slots, wide_pheno, pair, gram, system_hi, system_lo, cross, plain, totals, square,
    estimate, residual, direction, split, image, turned, pred, moved, packed, reduced,
    slot_send, slot_recv, forward_send, pair_send, pair_recv,
    pred_send, pred_recv, red_send, red_recv,
):
    depth, lines, share, half, pitch, people = sizes
    rows, block = dosage.shape
    columns = estimate.shape[1]
    train_count = float(people - people // FOLDS)
    z = lax.axis_index("people")
    x = lax.axis_index("blocks")
    core = lax.axis_index("sub")
    other = 1 - core
    total = depth * lines * 2
    me = (z * lines + x) * 2 + core

    barrier = pltpu.get_barrier_semaphore()

    @pl.loop(0, total)
    def _(index):
        @pl.when(index != me)
        def _():
            pl.semaphore_signal(
                barrier, inc=1,
                device_id={
                    "people": index // (lines * 2),
                    "blocks": (index // 2) % lines,
                    "sub": index % 2,
                },
                device_id_type=MESH,
            )

    mine = 2 * z + core
    slots[mine, pl.ds(0, block), :] = (
        jnp.transpose((dosage[...] - 100).astype(F32)).astype(BF16)
    )
    wide_pheno[...] = jnp.zeros_like(wide_pheno)
    wide_pheno[:, 0:TRAITS] = pheno[...].astype(F32)
    row = lax.broadcasted_iota(jnp.int32, (AUX, rows), 0)
    aux = jnp.where(
        row == FOLD_ROW,
        fold[...].astype(F32),
        jnp.where(row == ONE_ROW, 1.0, jnp.transpose(wide_pheno[...])[0:AUX, :]),
    ).astype(BF16)
    slots[mine, pl.ds(block, AUX), :] = aux
    pair[core] = aux
    pl.semaphore_wait(barrier, total - 1)

    first = depth // 2 - 1
    near = (z >= depth // 2).astype(jnp.int32)

    stretch = (block + AUX) // PIECES

    def slot_copies(place, send_sem, target):
        copies = []
        for piece in range(PIECES):
            part = slots.at[place, pl.ds(piece * stretch, stretch), :]
            copies.append(
                pltpu.make_async_remote_copy(
                    src_ref=part, dst_ref=part,
                    send_sem=send_sem.at[piece], recv_sem=slot_recv.at[place, piece],
                    device_id=target, device_id_type=MESH,
                )
            )
        return copies

    pair_copy = pltpu.make_async_remote_copy(
        src_ref=pair.at[core], dst_ref=pair.at[core],
        send_sem=pair_send, recv_sem=pair_recv,
        device_id={"sub": other}, device_id_type=MESH,
    )
    pair_copy.start()

    for order in range(2):
        goal = first + (near if order == 0 else 1 - near)

        if order == 1:
            closest = first + near

            @pl.when(z != closest)
            def _():
                for copy in slot_copies(mine, slot_send.at[0], {"people": closest}):
                    copy.wait_send()

        @pl.when(z != goal)
        def _():
            for copy in slot_copies(mine, slot_send.at[order], {"people": goal}):
                copy.start()

    solver = z - first
    is_solver = (solver >= 0) & (solver < 2)

    def pred_copy(far, group):
        return pltpu.make_async_remote_copy(
            src_ref=pred.at[far, pl.ds(group * pitch, pitch), :],
            dst_ref=moved.at[x, solver, core],
            send_sem=pred_send.at[far, group],
            recv_sem=pred_recv.at[x, solver, core],
            device_id={"people": far, "blocks": group // 2, "sub": group % 2},
            device_id_type=MESH,
        )

    @pl.when(is_solver)
    def _():
        gram[...] = jnp.zeros_like(gram)
        cross[...] = jnp.zeros_like(cross)
        plain[...] = jnp.zeros_like(plain)
        totals[...] = jnp.zeros_like(totals)
        square[...] = jnp.zeros_like(square)
        sign = 1 - 2 * solver

        @pl.loop(0, 2 * depth)
        def _(step):
            turn = step // 2
            late = step % 2
            far = z + sign * ((turn + 1) // 2) * (2 * (turn % 2) - 1)
            place = 2 * far + jnp.where(late == 0, core, other)
            for copy in slot_copies(place, forward_send.at[far], {"sub": other}):

                @pl.when(step > 0)
                def _():
                    copy.wait_recv()

                @pl.when(late == 0)
                def _():
                    copy.start()

            extra = slots[place, pl.ds(block, AUX), :]
            tail = slots[place, pl.ds(block + FOLD_ROW, AUX - FOLD_ROW), :]
            keep = (tail[0:1, :].astype(F32) != core.astype(F32)).astype(F32).astype(BF16)
            whole = slots[place, pl.ds(0, block), :]
            tile = 256
            for part in range(block // tile):
                span = pl.ds(part * tile, tile)
                own = slots[place, span, :]
                masked = own * keep
                gram[span, :] += dot_nt(masked, whole)
                cross[span, :] += dot_nt(masked, extra)
                plain[span, :] += dot_nt(own, extra)
                wide = own.astype(F32)
                wide = wide * wide
                added = wide[:, 0:128]
                for lane in range(1, rows // 128):
                    added = added + wide[:, lane * 128:(lane + 1) * 128]
                square[span, :] += added
            totals[...] += dot_nt(tail * keep, extra)

        one = ONE_ROW - FOLD_ROW
        lane = lax.broadcasted_iota(jnp.int32, (block, 128), 1)
        table = jnp.where(
            lane == 0,
            cross[:, ONE_ROW:ONE_ROW + 1],
            jnp.where(
                lane == 1,
                plain[:, ONE_ROW:ONE_ROW + 1],
                jnp.sum(square[...], 1, keepdims=True),
            ),
        )
        table = jnp.transpose(table)
        mean_row = table[1:2, :] / people
        train_row = table[0:1, :]
        square_row = table[2:3, :]
        inverse_row = 1.0 / jnp.sqrt(square_row / people - mean_row * mean_row + 1e-05)
        shifted_row = train_row - train_count * mean_row
        pick = (
            lax.broadcasted_iota(jnp.int32, (AUX, columns), 0)
            == colinfo[0:1, :] + solver * half
        ).astype(F32)
        which = colinfo[1:2, :]
        shifts = jnp.zeros((1, columns), F32)
        for ridge in range(RIDGES):
            shifts = shifts + jnp.where(which == ridge, ridges[ridge], 0.0)
        totals_row = jnp.dot(
            totals[...], pick, precision=highest, preferred_element_type=F32
        )[one:one + 1, :]
        tile = 128
        current = jnp.zeros((1, columns), F32)
        for part in range(block // tile):
            span = pl.ds(part * tile, tile)
            mean_col = plain[span, ONE_ROW:ONE_ROW + 1] / people
            train_col = cross[span, ONE_ROW:ONE_ROW + 1]
            square_col = jnp.sum(square[span, :], 1, keepdims=True)
            spread_col = jnp.sqrt(square_col / people - mean_col * mean_col + 1e-05)
            scale_col = 1.0 / (train_count * spread_col)
            value = gram[span, :] - train_col * mean_row - mean_col * shifted_row
            value = value * scale_col * inverse_row
            high = value.astype(BF16)
            system_hi[span, :] = high
            system_lo[span, :] = (value - high.astype(F32)).astype(BF16)
            right = jnp.dot(
                cross[span, :], pick, precision=highest, preferred_element_type=F32
            )
            right = (right - mean_col * totals_row) * scale_col
            residual[span, :] = right
            direction[span, :] = right
            estimate[span, :] = jnp.zeros_like(right)
            high = right.astype(BF16)
            split[span, 0:columns] = high
            split[span, columns:2 * columns] = (right - high.astype(F32)).astype(BF16)
            current = current + jnp.sum(right * right, 0, keepdims=True)

        tile = 256

        def step(exact, _, current):
            both = split[...] if exact else None
            leading = split[:, 0:columns]
            curve = jnp.zeros((1, columns), F32)
            for part in range(block // tile):
                span = pl.ds(part * tile, tile)
                along = direction[span, :]
                if exact:
                    wide = jnp.dot(system_hi[span, :], both, preferred_element_type=F32)
                    narrow = jnp.dot(system_lo[span, :], leading, preferred_element_type=F32)
                    value = wide[:, 0:columns] + (wide[:, columns:] + narrow)
                else:
                    value = jnp.dot(system_hi[span, :], leading, preferred_element_type=F32)
                value = value + shifts * along
                image[span, :] = value
                curve = curve + jnp.sum(along * value, 0, keepdims=True)
            alpha = current / curve
            following = jnp.zeros((1, columns), F32)
            for part in range(block // tile):
                span = pl.ds(part * tile, tile)
                left = residual[span, :] - alpha * image[span, :]
                residual[span, :] = left
                following = following + jnp.sum(left * left, 0, keepdims=True)
            ratio = following / current
            for part in range(block // tile):
                span = pl.ds(part * tile, tile)
                along = direction[span, :]
                estimate[span, :] += alpha * along
                along = residual[span, :] + ratio * along
                direction[span, :] = along
                high = along.astype(BF16)
                split[span, 0:columns] = high
                if exact:
                    split[span, columns:2 * columns] = (along - high.astype(F32)).astype(BF16)
            return following

        current = lax.fori_loop(0, EXACT, functools.partial(step, True), current)
        lax.fori_loop(EXACT, ITERS, functools.partial(step, False), current)

        for part in range(block // tile):
            span = pl.ds(part * tile, tile)
            mean_col = plain[span, ONE_ROW:ONE_ROW + 1] / people
            square_col = jnp.sum(square[span, :], 1, keepdims=True)
            spread_col = jnp.sqrt(square_col / people - mean_col * mean_col + 1e-05)
            image[span, :] = estimate[span, :] / spread_col
        flipped = jnp.transpose(image[...]).astype(BF16)
        turned[...] = flipped
        offset = jnp.sum(flipped.astype(F32) * mean_row, 1, keepdims=True)

        @pl.loop(0, depth)
        def _(turn):
            far = jnp.where(solver == 0, depth - 1 - turn, turn)
            for side in range(2):
                place = 2 * far + side
                outcome = jnp.dot(
                    turned[...], slots[place, pl.ds(0, block), :], preferred_element_type=F32
                )
                tail = slots[place, pl.ds(block + FOLD_ROW, AUX - FOLD_ROW), :]
                held = tail[0:1, :].astype(F32) == core.astype(F32)
                pred[far, :, side * rows:(side + 1) * rows] = jnp.where(
                    held, outcome - offset, 0.0
                ).astype(BF16)
            for group in range(2 * lines):
                self_here = (far == z) & (x == group // 2) & (core == group % 2)

                @pl.when(self_here)
                def _():
                    moved[x, solver, core] = pred[far, group * pitch:(group + 1) * pitch, :]

                @pl.when(jnp.logical_not(self_here))
                def _():
                    pred_copy(far, group).start()

    pair_copy.wait()
    for line in range(lines):
        for which_solver in range(2):
            for side in range(2):
                self_here = (z == first + which_solver) & (x == line) & (core == side)

                @pl.when(jnp.logical_not(self_here))
                def _():
                    pltpu.make_async_remote_copy(
                        src_ref=moved.at[line, which_solver, side],
                        dst_ref=moved.at[line, which_solver, side],
                        send_sem=red_send.at[0],
                        recv_sem=pred_recv.at[line, which_solver, side],
                        device_id={"sub": other}, device_id_type=MESH,
                    ).wait_recv()

    group = x * 2 + core
    choose = (
        (lax.broadcasted_iota(jnp.int32, (16, AUX), 1)
         == group * share + lax.broadcasted_iota(jnp.int32, (16, AUX), 0))
        & (lax.broadcasted_iota(jnp.int32, (16, AUX), 0) < share)
    ).astype(F32).astype(BF16)
    target = jnp.concatenate(
        [jnp.dot(choose, pair[side], preferred_element_type=F32) for side in range(2)], 1
    )
    predictors = []
    for line in range(lines):
        stacked = jnp.concatenate(
            [moved[line, which, 0] + moved[line, which, 1] for which in range(2)], 0
        )
        ordered = jnp.dot(perm[...], stacked, preferred_element_type=F32)
        for ridge in range(RIDGES):
            predictors.append(ordered[ridge * 16:(ridge + 1) * 16, :])
    count = len(predictors)
    pairs = [(a, b) for a in range(count) for b in range(a, count)]
    width = packed.shape[1]
    lane = lax.broadcasted_iota(jnp.int32, (16, width), 1)
    gathered = jnp.zeros((16, width), F32)
    for index, (a, b) in enumerate(pairs + [(a, None) for a in range(count)]):
        product = predictors[a] * (target if b is None else predictors[b])
        gathered = jnp.where(lane == index, jnp.sum(product, 1, keepdims=True), gathered)
    packed[...] = gathered

    def red_copy(far):
        return pltpu.make_async_remote_copy(
            src_ref=packed, dst_ref=reduced.at[z],
            send_sem=red_send.at[far], recv_sem=red_recv.at[z],
            device_id={"people": far}, device_id_type=MESH,
        )

    reduced[z] = gathered
    for far in range(depth):
        @pl.when(z != far)
        def _():
            red_copy(far).start()
    for far in range(depth):
        @pl.when(z != far)
        def _():
            pltpu.make_async_remote_copy(
                src_ref=packed, dst_ref=reduced.at[far],
                send_sem=red_send.at[far], recv_sem=red_recv.at[far],
                device_id={"people": far}, device_id_type=MESH,
            ).wait_recv()
    summed = reduced[0]
    for far in range(1, depth):
        summed = summed + reduced[far]
    summed = summed / people
    small = {}
    for index, (a, b) in enumerate(pairs):
        small[a, b] = jnp.broadcast_to(summed[:, index:index + 1], (16, 128))
        small[b, a] = small[a, b]
    level = small[0, 0]
    for a in range(1, count):
        level = level + small[a, a]
    level = level / count + 1e-06
    ridge_lane = lax.broadcasted_iota(jnp.int32, (16, 128), 1)
    ridge_row = jnp.zeros((16, 128), F32)
    for ridge in range(RIDGES):
        ridge_row = ridge_row + jnp.where(ridge_lane == ridge, ridges[ridge], 0.0)
    lift = level * ridge_row
    base = len(pairs)
    left = [
        jnp.broadcast_to(summed[:, base + a:base + a + 1], (16, 128)) for a in range(count)
    ]
    along = list(left)
    gamma = [jnp.zeros((16, 128), F32) for _ in range(count)]
    now = sum(v * v for v in left)
    for _ in range(ITERS_TWO):
        result = [
            sum(small[a, b] * along[b] for b in range(count)) + lift * along[a]
            for a in range(count)
        ]
        alpha = now / sum(along[a] * result[a] for a in range(count))
        gamma = [gamma[a] + alpha * along[a] for a in range(count)]
        left = [left[a] - alpha * result[a] for a in range(count)]
        later = sum(v * v for v in left)
        ratio = later / now
        along = [left[a] + ratio * along[a] for a in range(count)]
        now = later
    for ridge in range(RIDGES):
        value = predictors[0] * gamma[0][:, ridge:ridge + 1]
        for a in range(1, count):
            value = value + predictors[a] * gamma[a][:, ridge:ridge + 1]
        out[ridge] = value

    furthest = first + 1 - near

    @pl.when(z != furthest)
    def _():
        for copy in slot_copies(mine, slot_send.at[1], {"people": furthest}):
            copy.wait_send()

    for far in range(depth):
        @pl.when(z != far)
        def _():
            red_copy(far).wait_send()

    @pl.when(is_solver)
    def _():
        @pl.loop(0, depth)
        def _(far):
            for copy in slot_copies(2 * far + core, forward_send.at[far], {"sub": other}):
                copy.wait_send()
            for group in range(2 * lines):
                self_here = (far == z) & (x == group // 2) & (core == group % 2)

                @pl.when(jnp.logical_not(self_here))
                def _():
                    pred_copy(far, group).wait_send()


def shards(dosage, fold, pheno, ridges):
    rows, block = dosage.shape
    depth = lax.axis_size("people")
    lines = lax.axis_size("blocks")
    people = rows * depth * 2
    groups = lines * 2
    share = TRAITS // groups
    half = share // 2
    pitch = -(-RIDGES * half // 16) * 16
    columns = groups * pitch
    info = np.zeros((8, columns), np.int32)
    perm = np.zeros((RIDGES * 16, 2 * pitch), np.float32)
    for group in range(groups):
        for within in range(pitch):
            ridge, local = divmod(within, half) if within < RIDGES * half else (0, 0)
            info[0, group * pitch + within] = group * share + local
            info[1, group * pitch + within] = ridge
    for which in range(2):
        for within in range(RIDGES * half):
            ridge, local = divmod(within, half)
            perm[ridge * 16 + which * half + local, which * pitch + within] = 1.0
    count = lines * RIDGES
    width = -(-(count * (count + 1) // 2 + count) // 128) * 128
    vmem = pl.BlockSpec(memory_space=pltpu.VMEM)
    dma = pltpu.SemaphoreType.DMA
    result = pl.pallas_call(
        functools.partial(kernel, (depth, lines, share, half, pitch, people)),
        out_shape=jax.ShapeDtypeStruct((RIDGES, 16, 2 * rows), F32),
        in_specs=[vmem, vmem, vmem, vmem, vmem, pl.BlockSpec(memory_space=pltpu.SMEM)],
        out_specs=vmem,
        scratch_shapes=[
            pltpu.VMEM((2 * depth, block + AUX, rows), BF16),
            pltpu.VMEM((rows, 128), F32),
            pltpu.VMEM((2, AUX, rows), BF16),
            pltpu.VMEM((block, block), F32),
            pltpu.VMEM((block, block), BF16),
            pltpu.VMEM((block, block), BF16),
            pltpu.VMEM((block, AUX), F32),
            pltpu.VMEM((block, AUX), F32),
            pltpu.VMEM((AUX - FOLD_ROW, AUX), F32),
            pltpu.VMEM((block, 128), F32),
            pltpu.VMEM((block, columns), F32),
            pltpu.VMEM((block, columns), F32),
            pltpu.VMEM((block, columns), F32),
            pltpu.VMEM((block, 2 * columns), BF16),
            pltpu.VMEM((block, columns), F32),
            pltpu.VMEM((columns, block), BF16),
            pltpu.VMEM((depth, columns, 2 * rows), BF16),
            pltpu.VMEM((lines, 2, 2, pitch, 2 * rows), BF16),
            pltpu.VMEM((16, width), F32),
            pltpu.VMEM((depth, 16, width), F32),
            dma((2, PIECES)),
            dma((2 * depth, PIECES)),
            dma((depth, PIECES)),
            dma,
            dma,
            dma((depth, groups)),
            dma((lines, 2, 2)),
            dma((depth,)),
            dma((depth,)),
        ],
        compiler_params=pltpu.CompilerParams(
            collective_id=0, has_side_effects=True, vmem_limit_bytes=56 * 1024 * 1024
        ),
    )(dosage, fold[None, :], pheno, jnp.asarray(info), jnp.asarray(perm, BF16), ridges)
    return jnp.transpose(result[:, :share, :], (1, 0, 2))


def solution(mesh):
    return jax.shard_map(
        shards,
        mesh=mesh,
        in_specs=(
            P(("groups", "people", "sub"), "blocks"),
            P(("groups", "people", "sub")),
            P(("groups", "people", "sub"), None),
            P(),
        ),
        out_specs=P(("blocks", "sub"), None, ("groups", "people")),
        check_vma=False,
    )
```

```python
import functools

import jax
import jax.numpy as jnp
import numpy as np
from jax import lax
from jax.experimental import pallas as pl
from jax.experimental.pallas import tpu as pltpu
from jax.sharding import PartitionSpec as P

TRAITS = 48
RIDGES = 5
FOLDS = 2
ITERS = 10
ITERS_TWO = 4
EXACT = 4
PIECES = 4
AUX = 64
FOLD_ROW = 48
ONE_ROW = 49

MESH = pl.DeviceIdType.MESH
F32 = jnp.float32
BF16 = jnp.bfloat16
NT = (((1,), (1,)), ((), ()))
highest = lax.Precision.HIGHEST


def dot_nt(left, right, precision=None):
    return lax.dot_general(left, right, NT, precision=precision, preferred_element_type=F32)


def kernel(
    sizes,
    dosage, fold, pheno, colinfo, perm, ridges,
    out,
    slots, wide_pheno, pair, gram, system_hi, system_lo, cross, plain, totals, square,
    estimate, residual, direction, split, image, turned, pred, moved, packed, reduced,
    slot_send, slot_recv, forward_send, pair_send, pair_recv,
    pred_send, pred_recv, red_send, red_recv,
):
    depth, lines, share, half, pitch, people = sizes
    rows, block = dosage.shape
    columns = estimate.shape[1]
    train_count = float(people - people // FOLDS)
    z = lax.axis_index("people")
    x = lax.axis_index("blocks")
    core = lax.axis_index("sub")
    other = 1 - core
    total = depth * lines * 2
    me = (z * lines + x) * 2 + core

    barrier = pltpu.get_barrier_semaphore()

    @pl.loop(0, total)
    def _(index):
        @pl.when(index != me)
        def _():
            pl.semaphore_signal(
                barrier, inc=1,
                device_id={
                    "people": index // (lines * 2),
                    "blocks": (index // 2) % lines,
                    "sub": index % 2,
                },
                device_id_type=MESH,
            )

    mine = 2 * z + core
    slots[mine, pl.ds(0, block), :] = (
        jnp.transpose((dosage[...] - 100).astype(F32)).astype(BF16)
    )
    wide_pheno[...] = jnp.zeros_like(wide_pheno)
    wide_pheno[:, 0:TRAITS] = pheno[...].astype(F32)
    row = lax.broadcasted_iota(jnp.int32, (AUX, rows), 0)
    aux = jnp.where(
        row == FOLD_ROW,
        fold[...].astype(F32),
        jnp.where(row == ONE_ROW, 1.0, jnp.transpose(wide_pheno[...])[0:AUX, :]),
    ).astype(BF16)
    slots[mine, pl.ds(block, AUX), :] = aux
    pair[core] = aux
    pl.semaphore_wait(barrier, total - 1)

    first = depth // 2 - 1
    near = (z >= depth // 2).astype(jnp.int32)

    stretch = (block + AUX) // PIECES

    def slot_copies(place, send_sem, target):
        copies = []
        for piece in range(PIECES):
            part = slots.at[place, pl.ds(piece * stretch, stretch), :]
            copies.append(
                pltpu.make_async_remote_copy(
                    src_ref=part, dst_ref=part,
                    send_sem=send_sem.at[piece], recv_sem=slot_recv.at[place, piece],
                    device_id=target, device_id_type=MESH,
                )
            )
        return copies

    pair_copy = pltpu.make_async_remote_copy(
        src_ref=pair.at[core], dst_ref=pair.at[core],
        send_sem=pair_send, recv_sem=pair_recv,
        device_id={"sub": other}, device_id_type=MESH,
    )
    pair_copy.start()

    for order in range(2):
        goal = first + (near if order == 0 else 1 - near)

        if order == 1:
            closest = first + near

            @pl.when(z != closest)
            def _():
                for copy in slot_copies(mine, slot_send.at[0], {"people": closest}):
                    copy.wait_send()

        @pl.when(z != goal)
        def _():
            for copy in slot_copies(mine, slot_send.at[order], {"people": goal}):
                copy.start()

    solver = z - first
    is_solver = (solver >= 0) & (solver < 2)

    def pred_copy(far, group):
        return pltpu.make_async_remote_copy(
            src_ref=pred.at[far, pl.ds(group * pitch, pitch), :],
            dst_ref=moved.at[x, solver, core],
            send_sem=pred_send.at[far, group],
            recv_sem=pred_recv.at[x, solver, core],
            device_id={"people": far, "blocks": group // 2, "sub": group % 2},
            device_id_type=MESH,
        )

    @pl.when(is_solver)
    def _():
        gram[...] = jnp.zeros_like(gram)
        cross[...] = jnp.zeros_like(cross)
        plain[...] = jnp.zeros_like(plain)
        totals[...] = jnp.zeros_like(totals)
        square[...] = jnp.zeros_like(square)
        sign = 1 - 2 * solver

        @pl.loop(0, 2 * depth)
        def _(step):
            turn = step // 2
            late = step % 2
            far = z + sign * ((turn + 1) // 2) * (2 * (turn % 2) - 1)
            place = 2 * far + jnp.where(late == 0, core, other)
            for copy in slot_copies(place, forward_send.at[far], {"sub": other}):

                @pl.when(step > 0)
                def _():
                    copy.wait_recv()

                @pl.when(late == 0)
                def _():
                    copy.start()

            extra = slots[place, pl.ds(block, AUX), :]
            tail = slots[place, pl.ds(block + FOLD_ROW, AUX - FOLD_ROW), :]
            keep = (tail[0:1, :].astype(F32) != core.astype(F32)).astype(F32).astype(BF16)
            whole = slots[place, pl.ds(0, block), :]
            tile = 256
            for part in range(block // tile):
                span = pl.ds(part * tile, tile)
                own = slots[place, span, :]
                masked = own * keep
                gram[span, :] += dot_nt(masked, whole)
                cross[span, :] += dot_nt(masked, extra)
                plain[span, :] += dot_nt(own, extra)
                wide = own.astype(F32)
                wide = wide * wide
                added = wide[:, 0:128]
                for lane in range(1, rows // 128):
                    added = added + wide[:, lane * 128:(lane + 1) * 128]
                square[span, :] += added
            totals[...] += dot_nt(tail * keep, extra)

        one = ONE_ROW - FOLD_ROW
        lane = lax.broadcasted_iota(jnp.int32, (block, 128), 1)
        table = jnp.where(
            lane == 0,
            cross[:, ONE_ROW:ONE_ROW + 1],
            jnp.where(
                lane == 1,
                plain[:, ONE_ROW:ONE_ROW + 1],
                jnp.sum(square[...], 1, keepdims=True),
            ),
        )
        table = jnp.transpose(table)
        mean_row = table[1:2, :] / people
        train_row = table[0:1, :]
        square_row = table[2:3, :]
        inverse_row = 1.0 / jnp.sqrt(square_row / people - mean_row * mean_row + 1e-05)
        shifted_row = train_row - train_count * mean_row
        pick = (
            lax.broadcasted_iota(jnp.int32, (AUX, columns), 0)
            == colinfo[0:1, :] + solver * half
        ).astype(F32)
        which = colinfo[1:2, :]
        shifts = jnp.zeros((1, columns), F32)
        for ridge in range(RIDGES):
            shifts = shifts + jnp.where(which == ridge, ridges[ridge], 0.0)
        totals_row = jnp.dot(
            totals[...], pick, precision=highest, preferred_element_type=F32
        )[one:one + 1, :]
        tile = 128
        current = jnp.zeros((1, columns), F32)
        for part in range(block // tile):
            span = pl.ds(part * tile, tile)
            mean_col = plain[span, ONE_ROW:ONE_ROW + 1] / people
            train_col = cross[span, ONE_ROW:ONE_ROW + 1]
            square_col = jnp.sum(square[span, :], 1, keepdims=True)
            spread_col = jnp.sqrt(square_col / people - mean_col * mean_col + 1e-05)
            scale_col = 1.0 / (train_count * spread_col)
            value = gram[span, :] - train_col * mean_row - mean_col * shifted_row
            value = value * scale_col * inverse_row
            high = value.astype(BF16)
            system_hi[span, :] = high
            system_lo[span, :] = (value - high.astype(F32)).astype(BF16)
            right = jnp.dot(
                cross[span, :], pick, precision=highest, preferred_element_type=F32
            )
            right = (right - mean_col * totals_row) * scale_col
            residual[span, :] = right
            direction[span, :] = right
            estimate[span, :] = jnp.zeros_like(right)
            high = right.astype(BF16)
            split[span, 0:columns] = high
            split[span, columns:2 * columns] = (right - high.astype(F32)).astype(BF16)
            current = current + jnp.sum(right * right, 0, keepdims=True)

        tile = block // 2

        def step(exact, _, current):
            both = split[...] if exact else None
            leading = split[:, 0:columns]
            curve = jnp.zeros((1, columns), F32)
            for part in range(block // tile):
                span = pl.ds(part * tile, tile)
                along = direction[span, :]
                if exact:
                    wide = jnp.dot(system_hi[span, :], both, preferred_element_type=F32)
                    narrow = jnp.dot(system_lo[span, :], leading, preferred_element_type=F32)
                    value = wide[:, 0:columns] + (wide[:, columns:] + narrow)
                else:
                    value = jnp.dot(system_hi[span, :], leading, preferred_element_type=F32)
                value = value + shifts * along
                image[span, :] = value
                curve = curve + jnp.sum(along * value, 0, keepdims=True)
            alpha = current / curve
            following = jnp.zeros((1, columns), F32)
            for part in range(block // tile):
                span = pl.ds(part * tile, tile)
                left = residual[span, :] - alpha * image[span, :]
                residual[span, :] = left
                following = following + jnp.sum(left * left, 0, keepdims=True)
            ratio = following / current
            for part in range(block // tile):
                span = pl.ds(part * tile, tile)
                along = direction[span, :]
                estimate[span, :] += alpha * along
                along = residual[span, :] + ratio * along
                direction[span, :] = along
                high = along.astype(BF16)
                split[span, 0:columns] = high
                if exact:
                    split[span, columns:2 * columns] = (along - high.astype(F32)).astype(BF16)
            return following

        current = lax.fori_loop(0, EXACT, functools.partial(step, True), current)
        lax.fori_loop(EXACT, ITERS, functools.partial(step, False), current)

        for part in range(block // tile):
            span = pl.ds(part * tile, tile)
            mean_col = plain[span, ONE_ROW:ONE_ROW + 1] / people
            square_col = jnp.sum(square[span, :], 1, keepdims=True)
            spread_col = jnp.sqrt(square_col / people - mean_col * mean_col + 1e-05)
            image[span, :] = estimate[span, :] / spread_col
        flipped = jnp.transpose(image[...]).astype(BF16)
        turned[...] = flipped
        offset = jnp.sum(flipped.astype(F32) * mean_row, 1, keepdims=True)

        @pl.loop(0, depth)
        def _(turn):
            far = jnp.where(solver == 0, depth - 1 - turn, turn)
            for side in range(2):
                place = 2 * far + side
                outcome = jnp.dot(
                    turned[...], slots[place, pl.ds(0, block), :], preferred_element_type=F32
                )
                tail = slots[place, pl.ds(block + FOLD_ROW, AUX - FOLD_ROW), :]
                held = tail[0:1, :].astype(F32) == core.astype(F32)
                pred[far, :, side * rows:(side + 1) * rows] = jnp.where(
                    held, outcome - offset, 0.0
                ).astype(BF16)
            for group in range(2 * lines):
                self_here = (far == z) & (x == group // 2) & (core == group % 2)

                @pl.when(self_here)
                def _():
                    moved[x, solver, core] = pred[far, group * pitch:(group + 1) * pitch, :]

                @pl.when(jnp.logical_not(self_here))
                def _():
                    pred_copy(far, group).start()

    pair_copy.wait()
    for line in range(lines):
        for which_solver in range(2):
            for side in range(2):
                self_here = (z == first + which_solver) & (x == line) & (core == side)

                @pl.when(jnp.logical_not(self_here))
                def _():
                    pltpu.make_async_remote_copy(
                        src_ref=moved.at[line, which_solver, side],
                        dst_ref=moved.at[line, which_solver, side],
                        send_sem=red_send.at[0],
                        recv_sem=pred_recv.at[line, which_solver, side],
                        device_id={"sub": other}, device_id_type=MESH,
                    ).wait_recv()

    group = x * 2 + core
    choose = (
        (lax.broadcasted_iota(jnp.int32, (16, AUX), 1)
         == group * share + lax.broadcasted_iota(jnp.int32, (16, AUX), 0))
        & (lax.broadcasted_iota(jnp.int32, (16, AUX), 0) < share)
    ).astype(F32).astype(BF16)
    target = jnp.concatenate(
        [jnp.dot(choose, pair[side], preferred_element_type=F32) for side in range(2)], 1
    )
    predictors = []
    for line in range(lines):
        stacked = jnp.concatenate(
            [moved[line, which, 0] + moved[line, which, 1] for which in range(2)], 0
        )
        ordered = jnp.dot(perm[...], stacked, preferred_element_type=F32)
        for ridge in range(RIDGES):
            predictors.append(ordered[ridge * 16:(ridge + 1) * 16, :])
    count = len(predictors)
    pairs = [(a, b) for a in range(count) for b in range(a, count)]
    width = packed.shape[1]
    lane = lax.broadcasted_iota(jnp.int32, (16, width), 1)
    gathered = jnp.zeros((16, width), F32)
    for index, (a, b) in enumerate(pairs + [(a, None) for a in range(count)]):
        product = predictors[a] * (target if b is None else predictors[b])
        gathered = jnp.where(lane == index, jnp.sum(product, 1, keepdims=True), gathered)
    packed[...] = gathered

    def red_copy(far):
        return pltpu.make_async_remote_copy(
            src_ref=packed, dst_ref=reduced.at[z],
            send_sem=red_send.at[far], recv_sem=red_recv.at[z],
            device_id={"people": far}, device_id_type=MESH,
        )

    reduced[z] = gathered
    for far in range(depth):
        @pl.when(z != far)
        def _():
            red_copy(far).start()
    for far in range(depth):
        @pl.when(z != far)
        def _():
            pltpu.make_async_remote_copy(
                src_ref=packed, dst_ref=reduced.at[far],
                send_sem=red_send.at[far], recv_sem=red_recv.at[far],
                device_id={"people": far}, device_id_type=MESH,
            ).wait_recv()
    summed = reduced[0]
    for far in range(1, depth):
        summed = summed + reduced[far]
    summed = summed / people
    small = {}
    for index, (a, b) in enumerate(pairs):
        small[a, b] = jnp.broadcast_to(summed[:, index:index + 1], (16, 128))
        small[b, a] = small[a, b]
    level = small[0, 0]
    for a in range(1, count):
        level = level + small[a, a]
    level = level / count + 1e-06
    ridge_lane = lax.broadcasted_iota(jnp.int32, (16, 128), 1)
    ridge_row = jnp.zeros((16, 128), F32)
    for ridge in range(RIDGES):
        ridge_row = ridge_row + jnp.where(ridge_lane == ridge, ridges[ridge], 0.0)
    lift = level * ridge_row
    base = len(pairs)
    left = [
        jnp.broadcast_to(summed[:, base + a:base + a + 1], (16, 128)) for a in range(count)
    ]
    along = list(left)
    gamma = [jnp.zeros((16, 128), F32) for _ in range(count)]
    now = sum(v * v for v in left)
    for _ in range(ITERS_TWO):
        result = [
            sum(small[a, b] * along[b] for b in range(count)) + lift * along[a]
            for a in range(count)
        ]
        alpha = now / sum(along[a] * result[a] for a in range(count))
        gamma = [gamma[a] + alpha * along[a] for a in range(count)]
        left = [left[a] - alpha * result[a] for a in range(count)]
        later = sum(v * v for v in left)
        ratio = later / now
        along = [left[a] + ratio * along[a] for a in range(count)]
        now = later
    for ridge in range(RIDGES):
        value = predictors[0] * gamma[0][:, ridge:ridge + 1]
        for a in range(1, count):
            value = value + predictors[a] * gamma[a][:, ridge:ridge + 1]
        out[ridge] = value

    furthest = first + 1 - near

    @pl.when(z != furthest)
    def _():
        for copy in slot_copies(mine, slot_send.at[1], {"people": furthest}):
            copy.wait_send()

    for far in range(depth):
        @pl.when(z != far)
        def _():
            red_copy(far).wait_send()

    @pl.when(is_solver)
    def _():
        @pl.loop(0, depth)
        def _(far):
            for copy in slot_copies(2 * far + core, forward_send.at[far], {"sub": other}):
                copy.wait_send()
            for group in range(2 * lines):
                self_here = (far == z) & (x == group // 2) & (core == group % 2)

                @pl.when(jnp.logical_not(self_here))
                def _():
                    pred_copy(far, group).wait_send()


def shards(dosage, fold, pheno, ridges):
    rows, block = dosage.shape
    depth = lax.axis_size("people")
    lines = lax.axis_size("blocks")
    people = rows * depth * 2
    groups = lines * 2
    share = TRAITS // groups
    half = share // 2
    pitch = -(-RIDGES * half // 16) * 16
    columns = groups * pitch
    info = np.zeros((8, columns), np.int32)
    perm = np.zeros((RIDGES * 16, 2 * pitch), np.float32)
    for group in range(groups):
        for within in range(pitch):
            ridge, local = divmod(within, half) if within < RIDGES * half else (0, 0)
            info[0, group * pitch + within] = group * share + local
            info[1, group * pitch + within] = ridge
    for which in range(2):
        for within in range(RIDGES * half):
            ridge, local = divmod(within, half)
            perm[ridge * 16 + which * half + local, which * pitch + within] = 1.0
    count = lines * RIDGES
    width = -(-(count * (count + 1) // 2 + count) // 128) * 128
    vmem = pl.BlockSpec(memory_space=pltpu.VMEM)
    dma = pltpu.SemaphoreType.DMA
    result = pl.pallas_call(
        functools.partial(kernel, (depth, lines, share, half, pitch, people)),
        out_shape=jax.ShapeDtypeStruct((RIDGES, 16, 2 * rows), F32),
        in_specs=[vmem, vmem, vmem, vmem, vmem, pl.BlockSpec(memory_space=pltpu.SMEM)],
        out_specs=vmem,
        scratch_shapes=[
            pltpu.VMEM((2 * depth, block + AUX, rows), BF16),
            pltpu.VMEM((rows, 128), F32),
            pltpu.VMEM((2, AUX, rows), BF16),
            pltpu.VMEM((block, block), F32),
            pltpu.VMEM((block, block), BF16),
            pltpu.VMEM((block, block), BF16),
            pltpu.VMEM((block, AUX), F32),
            pltpu.VMEM((block, AUX), F32),
            pltpu.VMEM((AUX - FOLD_ROW, AUX), F32),
            pltpu.VMEM((block, 128), F32),
            pltpu.VMEM((block, columns), F32),
            pltpu.VMEM((block, columns), F32),
            pltpu.VMEM((block, columns), F32),
            pltpu.VMEM((block, 2 * columns), BF16),
            pltpu.VMEM((block, columns), F32),
            pltpu.VMEM((columns, block), BF16),
            pltpu.VMEM((depth, columns, 2 * rows), BF16),
            pltpu.VMEM((lines, 2, 2, pitch, 2 * rows), BF16),
            pltpu.VMEM((16, width), F32),
            pltpu.VMEM((depth, 16, width), F32),
            dma((2, PIECES)),
            dma((2 * depth, PIECES)),
            dma((depth, PIECES)),
            dma,
            dma,
            dma((depth, groups)),
            dma((lines, 2, 2)),
            dma((depth,)),
            dma((depth,)),
        ],
        compiler_params=pltpu.CompilerParams(
            collective_id=0, has_side_effects=True, vmem_limit_bytes=56 * 1024 * 1024
        ),
    )(dosage, fold[None, :], pheno, jnp.asarray(info), jnp.asarray(perm, BF16), ridges)
    return jnp.transpose(result[:, :share, :], (1, 0, 2))


def solution(mesh):
    return jax.shard_map(
        shards,
        mesh=mesh,
        in_specs=(
            P(("groups", "people", "sub"), "blocks"),
            P(("groups", "people", "sub")),
            P(("groups", "people", "sub"), None),
            P(),
        ),
        out_specs=P(("blocks", "sub"), None, ("groups", "people")),
        check_vma=False,
    )
```
